256 devices in a mesh: view: 8 (over y, x_lo), tok: 32 (over x_hi, z, core).
Axes of the slice: x: 4 (x_hi: 2, x_lo: 2; x = x_hi * 2 + x_lo), y: 4, z: 8, core: 2. Of those that a mesh axis runs over, the one named last changes fastest.
Arguments:
- queries: bfloat16 [8, 4096, 128], P('view', 'tok'), may hold values from -32 to 32
- keys: bfloat16 [8, 4096, 128], P('view', 'tok'), may hold values from -12 to 12
- values: bfloat16 [8, 4096, 128], P('view', 'tok'), may hold values from -6 to 6
- out_grad: bfloat16 [8, 4096, 128], P('view', 'tok'), may hold values from -24 to 24
- poses: float32 [16, 4, 4], replicated, may hold values from -1 to 1, as said below
- pose_index: int32 [8], replicated, may hold values from 0 to 15
Outputs:
- query_grad: bfloat16 [8, 4096, 128], P('view', 'tok')
- key_grad: bfloat16 [8, 4096, 128], P('view', 'tok')
- value_grad: bfloat16 [8, 4096, 128], P('view', 'tok')
The draws below stay inside these ranges and needn't reach their ends.
Inputs may be any that keep to these rules, and one draw needn't show every extreme that they name: `poses`: each row of the table is a rigid motion: a rotation in the upper left 3 x 3 block, a translation in the upper right column, and the bottom row 0 0 0 1.
All inputs are finite; a program needn't handle non-finite values.
Results may differ from the reference program's by a relative error of at most 0.022.
The reference program's roundings to bfloat16 on the way count: a program that leaves them out, or rounds other values in their place, can miss the bound.
Values may be sent and summed in bfloat16 or wider, within the bound.
A program may use at most 64 MiB of HBM per device.

```python
import math
import jax
import jax.numpy as jnp
from jax import lax

HD = 128
POSES = 16
VIEWS = 8
TPV = 4096


def paired_bases(key):
    query_key, key_key = jax.random.split(key)
    shape = (VIEWS, TPV, HD)
    query_base = jax.random.truncated_normal(query_key, -4.0, 4.0, shape, jnp.float32)
    key_base = jax.random.truncated_normal(key_key, -4.0, 4.0, shape, jnp.float32)
    return (query_base, key_base)


def draw_queries(key, part):
    query_base, key_base = paired_bases(key)
    queries = 2.5 * query_base
    return queries.astype(jnp.bfloat16)


def draw_keys(key, part):
    query_base, key_base = paired_bases(key)
    keys = key_base
    return keys.astype(jnp.bfloat16)


def draw_poses(key, part):
    key = jax.random.fold_in(key, 7)
    angle_key, shift_key = jax.random.split(key)
    angles = jax.random.uniform(angle_key, (3, POSES), jnp.float32, -math.pi, math.pi)
    shifts = jax.random.uniform(shift_key, (3, POSES), jnp.float32, -1.0, 1.0)
    cos_yaw, sin_yaw = (jnp.cos(angles[0]), jnp.sin(angles[0]))
    cos_pitch, sin_pitch = (jnp.cos(angles[1]), jnp.sin(angles[1]))
    cos_roll, sin_roll = (jnp.cos(angles[2]), jnp.sin(angles[2]))
    nought = jnp.zeros((POSES,), jnp.float32)
    unity = jnp.ones((POSES,), jnp.float32)
    first_row = jnp.stack([cos_yaw * cos_pitch, cos_yaw * sin_pitch * sin_roll - sin_yaw * cos_roll, cos_yaw * sin_pitch * cos_roll + sin_yaw * sin_roll, shifts[0]], axis=-1)
    second_row = jnp.stack([sin_yaw * cos_pitch, sin_yaw * sin_pitch * sin_roll + cos_yaw * cos_roll, sin_yaw * sin_pitch * cos_roll - cos_yaw * sin_roll, shifts[1]], axis=-1)
    third_row = jnp.stack([-sin_pitch, cos_pitch * sin_roll, cos_pitch * cos_roll, shifts[2]], axis=-1)
    last_row = jnp.stack([nought, nought, nought, unity], axis=-1)
    return jnp.stack([first_row, second_row, third_row, last_row], axis=1)


def with_ends(values, stream_key, least, largest):
    spot = [jax.random.randint(jax.random.fold_in(stream_key, axis), (), 0, length) for axis, length in enumerate(values.shape)]
    widest = values.shape.index(max(values.shape))
    neighbour = spot[:widest] + [(spot[widest] + 1) % values.shape[widest]] + spot[widest + 1:]
    return values.at[tuple(spot)].set(least).at[tuple(neighbour)].set(largest)


def level_of(rng, dims, cuts, smallest, largest):
    level = 1.0
    for axis_at, parts in cuts:
        steps = jax.random.uniform(jax.random.fold_in(jax.random.fold_in(rng, 6), axis_at), (parts,), jnp.float32, smallest / len(cuts), largest / len(cuts))
        level = level * jnp.repeat(jnp.exp(steps), dims[axis_at] // parts).reshape((-1,) + (1,) * (len(dims) - 1 - axis_at))
    return level


def centred(rng, shape, width, reach, cuts=(), kind=jnp.bfloat16):
    entries = jax.random.normal(rng, shape, jnp.float32) * width
    if len(cuts) > 0:
        entries = level_of(rng, shape, cuts, -0.22, 0.18) * entries
    return jnp.clip(entries, min=-reach, max=reach).astype(kind)


def setup_inputs(seed: int = 0) -> dict:
    key_of = jax.random.split(jax.random.key(seed), 7)
    queries = draw_queries(jax.random.fold_in(key_of[6], 71), 0)
    keys = draw_keys(jax.random.fold_in(key_of[6], 71), 0)
    values = centred(key_of[2], (VIEWS, TPV, HD), 1.0, 6.0, ((0, 8), (1, 32)))
    out_grad = centred(key_of[3], (VIEWS, TPV, HD), 4.0, 24.0, ((0, 8), (1, 32)))
    poses = draw_poses(jax.random.fold_in(key_of[6], 71), 0)
    pose_index = with_ends(jax.random.randint(key_of[5], (VIEWS,), 0, POSES), jax.random.fold_in(key_of[5], 1), 0, POSES - 1).astype(jnp.int32)
    return dict(queries=queries, keys=keys, values=values, out_grad=out_grad, poses=poses, pose_index=pose_index)


def inverse_pose(matrix):
    rotation = matrix[:3, :3].T
    shifted = -jnp.dot(rotation, matrix[:3, 3], precision=lax.Precision.HIGHEST)
    top_rows = jnp.concatenate([rotation, shifted[:, None]], axis=1)
    return jnp.concatenate([top_rows, matrix[3:4, :]], axis=0)


def block_matrix(matrix, feature_dim):
    return jnp.kron(jnp.eye(feature_dim // 4, dtype=jnp.float32), matrix)


def forward_block(matrix):
    return block_matrix(matrix, HD)


def backward_block(matrix):
    return block_matrix(inverse_pose(matrix).T, HD)


def rounded(array):
    return lax.optimization_barrier(array.astype(jnp.bfloat16)).astype(jnp.float32)


def reference(queries, keys, values, out_grad, poses, pose_index):
    highest = lax.Precision.HIGHEST
    pose_mats = poses[pose_index]
    forward_tables = jax.vmap(forward_block)(pose_mats)
    backward_tables = jax.vmap(backward_block)(pose_mats)

    def turned(array, tables):
        moved = jnp.einsum("vtd,vde->vte", array.astype(jnp.float32), tables, precision=highest)
        return rounded(moved).reshape(-1, HD)

    query_t = turned(queries, forward_tables)
    key_t = turned(keys, backward_tables)
    value_t = turned(values, backward_tables)
    grad_t = turned(out_grad, forward_tables)
    row_total = VIEWS * TPV
    block_rows = math.gcd(row_total, 1024)
    block_count = row_total // block_rows
    score_scale = HD ** -0.5
    query_blocks = query_t.reshape(block_count, block_rows, HD)
    grad_blocks = grad_t.reshape(block_count, block_rows, HD)

    def statistics(pieces):
        query_block, grad_block = pieces
        scores = jnp.dot(query_block, key_t.T) * score_scale
        row_peak = jnp.max(scores, axis=1)
        weights = jnp.exp(scores - row_peak[:, None])
        row_mass = jnp.sum(weights, axis=1)
        slopes = jnp.dot(grad_block, value_t.T)
        row_moment = jnp.sum(weights * slopes, axis=1)
        return row_peak + jnp.log(row_mass), row_moment / row_mass

    log_mass, centre = lax.map(statistics, (query_blocks, grad_blocks))

    def accumulate(carry, pieces):
        key_acc, value_acc = carry
        query_block, grad_block, log_block, centre_block = pieces
        scores = jnp.dot(query_block, key_t.T) * score_scale
        probs = jnp.exp(scores - log_block[:, None])
        slopes = jnp.dot(grad_block, value_t.T)
        probs_half = rounded(probs)
        dscores_half = rounded(probs * (slopes - centre_block[:, None]))
        query_part = jnp.dot(dscores_half, key_t) * score_scale
        key_acc = key_acc + jnp.dot(dscores_half.T, query_block) * score_scale
        value_acc = value_acc + jnp.dot(probs_half.T, grad_block)
        return (key_acc, value_acc), query_part

    empty_grad = jnp.zeros((row_total, HD), jnp.float32)
    (key_acc, value_acc), query_parts = lax.scan(accumulate, (empty_grad, empty_grad), (query_blocks, grad_blocks, log_mass, centre))

    def unturned(array, tables):
        shaped = array.reshape(VIEWS, TPV, HD)
        return jnp.einsum("vtd,ved->vte", shaped, tables, precision=highest).astype(jnp.bfloat16)

    query_grad = unturned(query_parts, forward_tables)
    key_grad = unturned(key_acc, backward_tables)
    value_grad = unturned(value_acc, backward_tables)
    return (query_grad, key_grad, value_grad)
```

```python
import math

import jax
import jax.numpy as jnp
from jax import lax
from jax.experimental import pallas as pl
from jax.experimental.pallas import tpu as pltpu
from jax.sharding import PartitionSpec as P

F32 = jnp.float32
BF16 = jnp.bfloat16
MESH = pl.DeviceIdType.MESH
HD = 128
TOK = 128
XS, YS, ZS = 4, 4, 8
ROWS = XS * YS * TOK
COLS = ZS * 2 * TOK
SCALE = HD**-0.5
SCALE2 = SCALE / math.log(2.0)
SEMS = 56


def nt(a, b):
    return lax.dot_general(a, b, (((1,), (1,)), ((), ())), preferred_element_type=F32)


def nn(a, b):
    return lax.dot_general(a, b, (((1,), (0,)), ((), ())), preferred_element_type=F32)


def turned(a, b, b_dim):
    return lax.dot_general(
        a, b, (((1,), (b_dim,)), ((), ())),
        precision=lax.Precision.HIGHEST, preferred_element_type=F32,
    )


def tables(poses, pose_index, view):
    row = pose_index[view]
    mat = [[poses[row, i, j] for j in range(4)] for i in range(4)]
    back = [[mat[i][j] for j in range(3)] + [mat[3][i]] for i in range(3)]
    back.append(
        [-(mat[0][j] * mat[0][3] + mat[1][j] * mat[1][3] + mat[2][j] * mat[2][3]) for j in range(3)]
        + [mat[3][3]]
    )
    i = lax.broadcasted_iota(jnp.int32, (HD, HD), 0)
    j = lax.broadcasted_iota(jnp.int32, (HD, HD), 1)
    place = jnp.where(i // 4 == j // 4, (i % 4) * 4 + j % 4, 16)
    forward = jnp.zeros((HD, HD), F32)
    backward = jnp.zeros((HD, HD), F32)
    for a in range(4):
        for b in range(4):
            here = place == 4 * a + b
            forward = jnp.where(here, mat[a][b], forward)
            backward = jnp.where(here, back[a][b], backward)
    return forward, backward


def kernel(
    q_ref, k_ref, v_ref, g_ref, poses, pose_index, dq_ref, dk_ref, dv_ref,
    qb, gb, kv, sc, sl, st, stx, sty, dkf, dvf, dqt,
    pair_out, pair_in, ring_out, ring_in, qa, qa_in, qa_mid, qa_fin, qc, qc_in, qc_mid, qc_fin,
    fwd, bwd, send_sem, recv_sem,
):
    view = lax.axis_index("view")
    tok = lax.axis_index("tok")
    y = view // 2
    x = (tok // 16) * 2 + view % 2
    z = (tok // 2) % 8
    c = tok % 2
    taken = [0]
    pending = []

    def device(dx=0, dy=0, dz=0, dc=0):
        px, py, pz, pc = (x + dx) % XS, (y + dy) % YS, (z + dz) % ZS, (c + dc) % 2
        return (py * 2 + px % 2, ((px // 2) * ZS + pz) * 2 + pc)

    def copy(src, dst, to, arrives):
        n = taken[0]
        taken[0] += 1
        out = pltpu.make_async_remote_copy(
            src_ref=src, dst_ref=dst, send_sem=send_sem.at[n], recv_sem=recv_sem.at[n],
            device_id=to, device_id_type=MESH,
        )
        out.start()
        pending.append((src, send_sem.at[n]))
        return lambda: pltpu.make_async_copy(arrives, arrives, recv_sem.at[n]).wait()

    barrier = pltpu.get_barrier_semaphore()
    peers = [dict(dx=d) for d in (1, 2, 3)] + [dict(dy=d) for d in (1, 2, 3)]
    peers += [dict(dz=1), dict(dz=ZS - 1), dict(dc=1)]
    for peer in peers:
        pl.semaphore_signal(barrier, inc=1, device_id=device(**peer), device_id_type=MESH)

    forward, backward = tables(poses, pose_index, view)
    fwd[...] = forward
    bwd[...] = backward
    qb[y, x] = turned(q_ref[0].astype(F32), forward, 0).astype(BF16)
    gb[x, y] = turned(g_ref[0].astype(F32), forward, 0).astype(BF16)
    kv[z, c, 0] = turned(k_ref[0].astype(F32), backward, 0).astype(BF16)
    kv[z, c, 1] = turned(v_ref[0].astype(F32), backward, 0).astype(BF16)
    pl.semaphore_wait(barrier, len(peers))

    def zat(d):
        return (z + d + ZS) % ZS

    q_first = [copy(qb.at[y, x], qb.at[y, x], device(dx=d), qb.at[y, (x + XS - d) % XS]) for d in (1, 3, 2)]
    g_first = [copy(gb.at[x, y], gb.at[x, y], device(dy=d), gb.at[x, (y + YS - d) % YS]) for d in (1, 3, 2)]
    shared = [copy(kv.at[z, c], kv.at[z, c], device(dc=1), kv.at[z, 1 - c])]
    half = (slice(None), slice(None))

    def ring(t):
        if t < ZS // 2:
            right = copy(kv.at[zat(1 - t), c], kv.at[zat(1 - t), c], device(dz=1), kv.at[zat(-t), c])
            left = copy(kv.at[zat(t - 1), c], kv.at[zat(t - 1), c], device(dz=ZS - 1), kv.at[zat(t), c])
        else:
            right = copy(kv.at[zat(1 - t), c, 0], kv.at[zat(1 - t), c, 0], device(dz=1), kv.at[zat(-t), c, 0])
            left = copy(kv.at[zat(t - 1), c, 1], kv.at[zat(t - 1), c, 1], device(dz=ZS - 1), kv.at[zat(t), c, 1])
        return right, left

    def share(t):
        if t < ZS // 2:
            for w in (zat(-t), zat(t)):
                shared.append(copy(kv.at[w, c], kv.at[w, c], device(dc=1), kv.at[w, 1 - c]))
        else:
            for part, w in ((0, zat(-t)), (1, zat(t))):
                shared.append(copy(kv.at[w, c, part], kv.at[w, c, part], device(dc=1), kv.at[w, 1 - c, part]))

    arriving = ring(1)
    for t in range(1, ZS // 2 + 1):
        for wait in arriving:
            wait()
        if t < ZS // 2:
            arriving = ring(t + 1)
        share(t)
        if t == 1:
            for wait in q_first:
                wait()
            q_second = [copy(qb.at[y], qb.at[y], device(dy=d), qb.at[(y + YS - d) % YS]) for d in (1, 3, 2)]
            for wait in g_first:
                wait()
            g_second = [copy(gb.at[x], gb.at[x], device(dx=d), gb.at[(x + XS - d) % XS]) for d in (1, 3, 2)]
    for wait in shared + q_second + g_second:
        wait()

    keys = kv[:, :, 0].reshape(COLS, HD)
    vals = kv[:, :, 1].reshape(COLS, HD)

    def statistics(r, carry):
        ry, rx = r // XS, r % XS
        cols = pl.ds(pl.multiple_of(r * TOK, TOK), TOK)
        s = nt(kv[:, :, 0].reshape(COLS, HD), qb[ry, rx]) * SCALE2
        p = nt(kv[:, :, 1].reshape(COLS, HD), gb[rx, ry])
        sc[:, cols] = s
        sl[:, cols] = p
        s = s.reshape(COLS // 8, 8, TOK)
        peak = jnp.max(s, axis=0)
        w = jnp.exp2(s - peak[None])
        mass = jnp.sum(w, axis=0)
        moment = jnp.sum(w * p.reshape(COLS // 8, 8, TOK), axis=0)
        top = jnp.max(peak, axis=0, keepdims=True)
        factor = jnp.exp2(peak - top)
        mass = jnp.sum(mass * factor, axis=0, keepdims=True)
        moment = jnp.sum(moment * factor, axis=0, keepdims=True)
        st[0, pl.ds(r, 1), :] = top + jnp.log2(mass)
        st[1, pl.ds(r, 1), :] = moment / mass
        return carry

    lax.fori_loop(0, XS * YS, statistics, 0)

    def merge(parts):
        logs = [part[0] for part in parts]
        top = logs[0]
        for log in logs[1:]:
            top = jnp.maximum(top, log)
        weights = [jnp.exp2(log - top) for log in logs]
        mass = weights[0]
        moment = weights[0] * parts[0][1]
        for weight, part in zip(weights[1:], parts[1:]):
            mass = mass + weight
            moment = moment + weight * part[1]
        return top + jnp.log2(mass), moment / mass

    def exchange(source, landing, axis):
        waits = [copy(source, landing.at[d - 1], device(**{axis: d}), landing.at[d - 1]) for d in (1, 3, 2)]
        for wait in waits:
            wait()

    exchange(st, stx, "dx")
    log_mass, centre = merge([st] + [stx.at[d] for d in range(3)])
    sty[3, 0] = log_mass
    sty[3, 1] = centre
    exchange(sty.at[3], sty, "dy")
    log_mass, centre = merge([sty.at[3]] + [sty.at[d] for d in range(3)])
    st2 = stx.at[0]
    st2[0] = log_mass
    st2[1] = centre

    dqt[...] = jnp.zeros_like(dqt)

    def gradients(i, carry):
        cols = pl.ds(pl.multiple_of(i * 512, 512), 512)
        zs = pl.ds(i * 2, 2)
        kt = kv[zs, :, 0].reshape(512, HD).T
        dk = jnp.zeros((512, HD), F32)
        dv = jnp.zeros((512, HD), F32)
        for ry in range(YS):
            rows = slice(ry * 512, ry * 512 + 512)
            log_row = jnp.concatenate([st2[0, ry * 4 + n : ry * 4 + n + 1, :] for n in range(4)], axis=1)
            centre_row = jnp.concatenate([st2[1, ry * 4 + n : ry * 4 + n + 1, :] for n in range(4)], axis=1)
            probs = jnp.exp2(sc[cols, rows] - log_row)
            ds = (probs * (sl[cols, rows] - centre_row)).astype(BF16)
            dk = dk + nn(ds, qb[ry].reshape(512, HD))
            dv = dv + nn(probs.astype(BF16), gb[:, ry].reshape(512, HD))
            dqt[:, rows] += nn(kt, ds)
        dkf[zs] = dk.reshape(2, 2, TOK, HD)
        dvf[zs] = dv.reshape(2, 2, TOK, HD)
        return carry

    lax.fori_loop(0, COLS // 512, gradients, 0)

    for w in range(ZS):
        pair_out[w, 0] = dkf[w, 1 - c].astype(BF16)
        pair_out[w, 1] = dvf[w, 1 - c].astype(BF16)
    pair = copy(pair_out, pair_in, device(dc=1), pair_in)
    for ry in range(YS):
        for rx in range(XS):
            r = ry * XS + rx
            block = dqt[:, r * TOK : r * TOK + TOK].astype(BF16)
            qa[ry, rx] = block[: HD // 2]
            qc[rx, ry] = block[HD // 2 :]
    a_waits = [copy(qa.at[(y + d) % YS], qa_in.at[d - 1], device(dy=d), qa_in.at[d - 1]) for d in (1, 3, 2)]
    c_waits = [copy(qc.at[(x + d) % XS], qc_in.at[d - 1], device(dx=d), qc_in.at[d - 1]) for d in (1, 3, 2)]
    pair()

    def own(w, part):
        return (dkf, dvf)[part][w, c] + pair_in[w, part].astype(F32)

    last = ZS // 2
    for t in range(1, last + 1):
        far = last + 1 - t
        right_parts = (0,) if t == 1 else (0, 1)
        left_parts = (1,) if t == 1 else (0, 1)
        for way, w, parts in ((0, zat(far), right_parts), (1, zat(-far), left_parts)):
            for part in parts:
                total = own(w, part)
                if t > 2 or (t == 2 and part == way):
                    total = total + ring_in[way, t - 2, part].astype(F32)
                ring_out[way, t - 1, part] = total.astype(BF16)
        if t == 1:
            waits = [
                copy(ring_out.at[w, 0, w], ring_in.at[w, 0, w], device(dz=(1, ZS - 1)[w]), ring_in.at[w, 0, w])
                for w in (0, 1)
            ]
        else:
            waits = [
                copy(ring_out.at[w, t - 1], ring_in.at[w, t - 1], device(dz=(1, ZS - 1)[w]), ring_in.at[w, t - 1])
                for w in (0, 1)
            ]
        if t == 1:
            for wait in a_waits:
                wait()
            qa_mid[...] = (
                qa[y].astype(F32) + qa_in[0].astype(F32) + qa_in[1].astype(F32) + qa_in[2].astype(F32)
            ).astype(BF16)
            a_waits = [copy(qa_mid.at[(x + d) % XS], qa_fin.at[d - 1], device(dx=d), qa_fin.at[d - 1]) for d in (1, 3, 2)]
            for wait in c_waits:
                wait()
            qc_mid[...] = (
                qc[x].astype(F32) + qc_in[0].astype(F32) + qc_in[1].astype(F32) + qc_in[2].astype(F32)
            ).astype(BF16)
            c_waits = [copy(qc_mid.at[(y + d) % YS], qc_fin.at[d - 1], device(dy=d), qc_fin.at[d - 1]) for d in (1, 3, 2)]
        for wait in waits:
            wait()
    for wait in a_waits + c_waits:
        wait()
    dk = own(z, 0) + ring_in[0, last - 1, 0].astype(F32) + ring_in[1, last - 1, 0].astype(F32)
    dv = own(z, 1) + ring_in[0, last - 1, 1].astype(F32) + ring_in[1, last - 1, 1].astype(F32)
    top = qa_mid[x].astype(F32) + qa_fin[0].astype(F32) + qa_fin[1].astype(F32) + qa_fin[2].astype(F32)
    low = qc_mid[y].astype(F32) + qc_fin[0].astype(F32) + qc_fin[1].astype(F32) + qc_fin[2].astype(F32)
    dq = jnp.concatenate([top, low], axis=0).T
    dq_ref[0] = (turned(dq, fwd[...], 1) * SCALE).astype(BF16)
    dk_ref[0] = (turned(dk, bwd[...], 1) * SCALE).astype(BF16)
    dv_ref[0] = turned(dv, bwd[...], 1).astype(BF16)
    for src, sem in pending:
        pltpu.make_async_copy(src, src, sem).wait()
    assert taken[0] <= SEMS


def per_device(queries, keys, values, out_grad, poses, pose_index):
    block = jax.ShapeDtypeStruct((1, TOK, HD), BF16)
    vmem = pl.BlockSpec(memory_space=pltpu.VMEM)
    smem = pl.BlockSpec(memory_space=pltpu.SMEM)

    def buf(*shape, kind=BF16):
        return pltpu.VMEM(shape, kind)

    half = HD // 2
    return pl.pallas_call(
        kernel,
        out_shape=(block, block, block),
        in_specs=[vmem] * 4 + [smem] * 2,
        out_specs=(vmem, vmem, vmem),
        scratch_shapes=[
            buf(YS, XS, TOK, HD), buf(XS, YS, TOK, HD), buf(ZS, 2, 2, TOK, HD),
            buf(COLS, ROWS, kind=F32), buf(COLS, ROWS, kind=F32),
            buf(2, 16, TOK, kind=F32), buf(3, 2, 16, TOK, kind=F32), buf(4, 2, 16, TOK, kind=F32),
            buf(ZS, 2, TOK, HD, kind=F32), buf(ZS, 2, TOK, HD, kind=F32), buf(HD, ROWS, kind=F32),
            buf(ZS, 2, TOK, HD), buf(ZS, 2, TOK, HD),
            buf(2, 4, 2, TOK, HD), buf(2, 4, 2, TOK, HD),
            buf(YS, XS, half, TOK), buf(3, XS, half, TOK), buf(XS, half, TOK), buf(3, half, TOK),
            buf(XS, YS, half, TOK), buf(3, YS, half, TOK), buf(YS, half, TOK), buf(3, half, TOK),
            buf(HD, HD, kind=F32), buf(HD, HD, kind=F32),
            pltpu.SemaphoreType.DMA((SEMS,)), pltpu.SemaphoreType.DMA((SEMS,)),
        ],
        compiler_params=pltpu.CompilerParams(
            collective_id=0, has_side_effects=True, vmem_limit_bytes=58 * 2**20
        ),
    )(queries, keys, values, out_grad, poses, pose_index)


def solution(mesh):
    block = P("view", "tok", None)
    return jax.shard_map(
        per_device, mesh=mesh, in_specs=(block,) * 4 + (P(), P()), out_specs=(block,) * 3, check_vma=False
    )
```

```python
import math

import jax
import jax.numpy as jnp
from jax import lax
from jax.experimental import pallas as pl
from jax.experimental.pallas import tpu as pltpu
from jax.sharding import PartitionSpec as P

F32 = jnp.float32
BF16 = jnp.bfloat16
MESH = pl.DeviceIdType.MESH
HD = 128
TOK = 128
XS, YS, ZS = 4, 4, 8
ROWS = XS * YS * TOK
COLS = ZS * 2 * TOK
SCALE = HD**-0.5
SCALE2 = SCALE / math.log(2.0)
SEMS = 128
HALF = TOK // 2
LANES = ROWS // 2
DIST = (0, 1, -1, 2, -2, 3, -3, 4)
POS = {d: p for p, d in enumerate(DIST)}
UNROLL = 1
NEAR = 5


def nt(a, b):
    return lax.dot_general(a, b, (((1,), (1,)), ((), ())), preferred_element_type=F32)


def nn(a, b):
    return lax.dot_general(a, b, (((1,), (0,)), ((), ())), preferred_element_type=F32)


def turned(a, b, b_dim):
    return lax.dot_general(
        a, b, (((1,), (b_dim,)), ((), ())),
        precision=lax.Precision.HIGHEST, preferred_element_type=F32,
    )


def tables(poses, pose_index, view):
    row = pose_index[view]
    mat = [[poses[i, j, row] for j in range(4)] for i in range(4)]
    back = [[mat[i][j] for j in range(3)] + [mat[3][i]] for i in range(3)]
    back.append(
        [-(mat[0][j] * mat[0][3] + mat[1][j] * mat[1][3] + mat[2][j] * mat[2][3]) for j in range(3)]
        + [mat[3][3]]
    )
    i = lax.broadcasted_iota(jnp.int32, (HD, HD), 0)
    j = lax.broadcasted_iota(jnp.int32, (HD, HD), 1)
    place = jnp.where(i // 4 == j // 4, (i % 4) * 4 + j % 4, 16)
    forward = jnp.zeros((HD, HD), F32)
    backward = jnp.zeros((HD, HD), F32)
    for a in range(4):
        for b in range(4):
            here = place == 4 * a + b
            forward = jnp.where(here, mat[a][b], forward)
            backward = jnp.where(here, back[a][b], backward)
    return forward, backward


def kernel(
    q_ref, k_ref, v_ref, g_ref, poses, pose_index, dq_ref, dk_ref, dv_ref,
    qb, gb, kv, wt, sl, pk, ms, mo, st, stx, mid, sty, fs, cs, dkf, dvf, dqt,
    pair_out, pair_in, red_out, relay_out, red_in,
    qa, qa_in, qa_mid, qa_fin, qc, qc_in, qc_mid, qc_fin, fwd, bwd, send_sem, recv_sem,
):
    view = lax.axis_index("view")
    tok = lax.axis_index("tok")
    y = view // 2
    x = (tok // 16) * 2 + view % 2
    z = (tok // 2) % 8
    c = tok % 2
    taken = [0]
    pending = []

    def device(dx=0, dy=0, dz=0, dc=0):
        px, py, pz, pc = (x + dx) % XS, (y + dy) % YS, (z + dz + ZS) % ZS, (c + dc) % 2
        return (py * 2 + px % 2, ((px // 2) * ZS + pz) * 2 + pc)

    def copy(src, dst, to, arrives=None):
        n = taken[0]
        taken[0] += 1
        arrives = dst if arrives is None else arrives
        pltpu.make_async_remote_copy(
            src_ref=src, dst_ref=dst, send_sem=send_sem.at[n], recv_sem=recv_sem.at[n],
            device_id=device(**to), device_id_type=MESH,
        ).start()
        pending.append((src, send_sem.at[n]))
        return lambda: pltpu.make_async_copy(arrives, arrives, recv_sem.at[n]).wait()

    def done(waits):
        for wait in waits:
            wait()

    barrier = pltpu.get_barrier_semaphore()
    peers = [dict(dx=d) for d in (1, 2, 3)] + [dict(dy=d) for d in (1, 2, 3)]
    peers += [dict(dz=d) for d in (1, -1, 2, -2)] + [dict(dc=1)]
    for peer in peers:
        pl.semaphore_signal(barrier, inc=1, device_id=device(**peer), device_id_type=MESH)

    forward, backward = tables(poses, pose_index, view)
    fwd[...] = forward
    bwd[...] = backward
    kv[0, 0, 0] = turned(k_ref[0].astype(F32), backward, 0).astype(BF16)
    kv[0, 0, 1] = turned(v_ref[0].astype(F32), backward, 0).astype(BF16)
    q_own = turned(q_ref[0].astype(F32), forward, 0).astype(BF16)
    g_own = turned(g_ref[0].astype(F32), forward, 0).astype(BF16)
    for h in range(2):
        qb[h, y, x] = q_own[h * HALF : h * HALF + HALF]
        gb[h, x, y] = g_own[h * HALF : h * HALF + HALF]
    dqt[...] = jnp.zeros_like(dqt)
    pl.semaphore_wait(barrier, len(peers))

    ahead, behind = [None, None], [None, None]
    ahead[0] = copy(kv.at[0, 0, 0], kv.at[POS[-2], 0, 0], dict(dz=2))
    behind[1] = copy(kv.at[0, 0, 1], kv.at[POS[2], 0, 1], dict(dz=-2))
    q_first, g_first, q_second, g_second = [], [], [], []
    for h in range(2):
        q_first.append([
            copy(qb.at[h, y, x], qb.at[h, y, x], dict(dx=d), qb.at[h, y, (x + XS - d) % XS]) for d in (1, 3, 2)
        ])
        g_first.append([
            copy(gb.at[h, x, y], gb.at[h, x, y], dict(dy=d), gb.at[h, x, (y + YS - d) % YS]) for d in (1, 3, 2)
        ])
        if h == 0:
            ahead[1] = copy(kv.at[0, 0, 1], kv.at[POS[-2], 0, 1], dict(dz=2))
            behind[0] = copy(kv.at[0, 0, 0], kv.at[POS[2], 0, 0], dict(dz=-2))
    shared = [copy(kv.at[0, 0], kv.at[0, 1], dict(dc=1))]
    beside = [copy(kv.at[0, 0], kv.at[POS[-1], 0], dict(dz=1)), copy(kv.at[0, 0], kv.at[POS[1], 0], dict(dz=-1))]

    def share(p, part):
        return copy(kv.at[p, 0, part], kv.at[p, 1, part], dict(dc=1))

    for h in range(2):
        done(q_first[h])
        q_second.append([
            copy(qb.at[h, y], qb.at[h, y], dict(dy=d), qb.at[h, (y + YS - d) % YS]) for d in (1, 3, 2)
        ])
        done(g_first[h])
        g_second.append([
            copy(gb.at[h, x], gb.at[h, x], dict(dx=d), gb.at[h, (x + XS - d) % XS]) for d in (1, 3, 2)
        ])
        if h == 0:
            far = {}
            for part, way in ((0, 1), (1, -1)):
                (ahead, behind)[part][part]()
                p = POS[-2 * way]
                far[4, part] = copy(kv.at[p, 0, part], kv.at[POS[4], 0, part], dict(dz=2 * way))
                far[-3 * way, part] = copy(kv.at[p, 0, part], kv.at[POS[-3 * way], 0, part], dict(dz=way))
                shared.append(share(p, part))
    for part, way in ((1, 1), (0, -1)):
        (behind, ahead)[part][part]()
        p = POS[-2 * way]
        far[-3 * way, part] = copy(kv.at[p, 0, part], kv.at[POS[-3 * way], 0, part], dict(dz=way))
        shared.append(share(p, part))
    done(beside)
    for d in (1, -1):
        shared.append(copy(kv.at[POS[d], 0], kv.at[POS[d], 1], dict(dc=1)))
    done(shared)

    def scores(h, ch):
        lo, hi = ((0, NEAR), (NEAR, ZS))[ch]
        n = (hi - lo) * 256
        for i in range(LANES // TOK):
            ry, rx = i // 2, (i % 2) * 2
            lanes = slice(h * LANES + i * TOK, h * LANES + i * TOK + TOK)
            here = slice(i * TOK, i * TOK + TOK)
            s = nt(kv[lo:hi, :, 0].reshape(n, HD), qb[h, ry, rx : rx + 2].reshape(TOK, HD)) * SCALE2
            t = nt(kv[lo:hi, :, 1].reshape(n, HD), gb[h, rx : rx + 2, ry].reshape(TOK, HD))
            sl[lo * 256 : hi * 256, lanes] = t
            s = s.reshape(n // 8, 8, TOK)
            peak = jnp.max(s, axis=0)
            w = jnp.exp2(s - peak[None])
            wt[lo * 256 : hi * 256, lanes] = w.reshape(n, TOK)
            pk[h, ch, :, here] = peak
            ms[h, ch, :, here] = jnp.sum(w, axis=0)
            mo[h, ch, :, here] = jnp.sum(w * t.reshape(n // 8, 8, TOK), axis=0)

    def local_statistics(h):
        top = jnp.maximum(pk[h, 0], pk[h, 1])
        row_top = jnp.max(top, axis=0, keepdims=True)
        near, far_off = jnp.exp2(pk[h, 0] - row_top), jnp.exp2(pk[h, 1] - row_top)
        mass = jnp.sum(ms[h, 0] * near + ms[h, 1] * far_off, axis=0, keepdims=True)
        moment = jnp.sum(mo[h, 0] * near + mo[h, 1] * far_off, axis=0, keepdims=True)
        log_mass = row_top + jnp.log2(mass)
        centre = moment / mass
        for i in range(LANES // TOK):
            st[h, 0, i : i + 1, :] = log_mass[:, i * TOK : i * TOK + TOK]
            st[h, 1, i : i + 1, :] = centre[:, i * TOK : i * TOK + TOK]

    def merge(parts):
        logs = [part[0] for part in parts]
        top = logs[0]
        for log in logs[1:]:
            top = jnp.maximum(top, log)
        weights = [jnp.exp2(log - top) for log in logs]
        mass = weights[0]
        moment = weights[0] * parts[0][1]
        for weight, part in zip(weights[1:], parts[1:]):
            mass = mass + weight
            moment = moment + weight * part[1]
        return top + jnp.log2(mass), moment / mass

    def along_x(h):
        return [copy(st.at[h], stx.at[h, d - 1], dict(dx=d)) for d in (1, 3, 2)]

    def along_y(h, waits):
        done(waits)
        log_mass, centre = merge([st.at[h]] + [stx.at[h, d] for d in range(3)])
        mid[h, 0] = log_mass
        mid[h, 1] = centre
        return [copy(mid.at[h], sty.at[h, d - 1], dict(dy=d)) for d in (1, 3, 2)]

    def settle(h, waits):
        done(waits)
        log_mass, centre = merge([mid.at[h]] + [sty.at[h, d] for d in range(3)])
        for i in range(LANES // TOK):
            here = slice(i * TOK, i * TOK + TOK)
            cs[h, :, here] = centre[i : i + 1, :]
            for ch in range(2):
                fs[h, ch, :, here] = jnp.exp2(pk[h, ch, :, here] - log_mass[i : i + 1, :])

    done(q_second[0] + g_second[0])
    scores(0, 0)
    last_shared = []
    for d, part in ((4, 0), (4, 1), (-3, 0), (3, 1), (-3, 1), (3, 0)):
        far[d, part]()
        last_shared.append(share(POS[d], part))
    done(q_second[1] + g_second[1])
    scores(1, 0)
    done(last_shared)
    scores(0, 1)
    local_statistics(0)
    first_x = along_x(0)
    scores(1, 1)
    local_statistics(1)
    second_x = along_x(1)
    first_y = along_y(0, first_x)
    second_y = along_y(1, second_x)

    def gradients(h, lo, hi):
        def block(p, carry):
            ch = p // NEAR
            cols = pl.ds(pl.multiple_of(p * 256, 256), 256)
            kt = kv[p, :, 0].reshape(256, HD).T
            if h == 0:
                dk = jnp.zeros((256, HD), F32)
                dv = jnp.zeros((256, HD), F32)
            else:
                dk = dkf[p].reshape(256, HD)
                dv = dvf[p].reshape(256, HD)
            for ry in range(YS):
                here = slice(ry * 256, ry * 256 + 256)
                lanes = slice(h * LANES + ry * 256, h * LANES + ry * 256 + 256)
                w = wt[cols, lanes].reshape(32, 8, 256)
                probs = (w * fs[h, ch, :, here][None]).reshape(256, 256)
                ds = (probs * (sl[cols, lanes] - cs[h, :, here])).astype(BF16)
                dk = dk + nn(ds, qb[h, ry].reshape(256, HD))
                dv = dv + nn(probs.astype(BF16), gb[h, :, ry].reshape(256, HD))
                dqt[h, :, here] += nn(kt, ds)
            dkf[p] = dk.reshape(2, TOK, HD)
            dvf[p] = dv.reshape(2, TOK, HD)
            return carry

        lax.fori_loop(lo, hi, block, 0, unroll=UNROLL)

    def query_start(h):
        for i in range(LANES // TOK):
            rows = dqt[h, :, i * TOK : i * TOK + TOK].T.astype(BF16)
            for b in range(2):
                ry, rx = i // 2, (i % 2) * 2 + b
                qa[h, ry, rx] = rows[b * HALF : b * HALF + HALF // 2]
                qc[h, rx, ry] = rows[b * HALF + HALF // 2 : b * HALF + HALF]
        a = [copy(qa.at[h, (y + d) % YS], qa_in.at[h, d - 1], dict(dy=d)) for d in (1, 3, 2)]
        b = [copy(qc.at[h, (x + d) % XS], qc_in.at[h, d - 1], dict(dx=d)) for d in (1, 3, 2)]
        return a, b

    def four(mine, others):
        total = mine.astype(F32)
        for n in range(3):
            total = total + others[n].astype(F32)
        return total

    def query_second(h, waits):
        done(waits[0])
        qa_mid[h] = four(qa[h, y], qa_in[h]).astype(BF16)
        a = [copy(qa_mid.at[h, (x + d) % XS], qa_fin.at[h, d - 1], dict(dx=d)) for d in (1, 3, 2)]
        done(waits[1])
        qc_mid[h] = four(qc[h, x], qc_in[h]).astype(BF16)
        b = [copy(qc_mid.at[h, (y + d) % YS], qc_fin.at[h, d - 1], dict(dy=d)) for d in (1, 3, 2)]
        return a + b

    def query_sum(h, waits):
        done(waits)
        return [four(qa_mid[h, x], qa_fin[h]), four(qc_mid[h, y], qc_fin[h])]

    def pair(lo, hi):
        waits = []
        for part, total in enumerate((dkf, dvf)):
            pair_out[part, lo:hi] = total[lo:hi, 1].astype(BF16)
            waits.append(copy(pair_out.at[part, lo:hi], pair_in.at[part, lo:hi], dict(dc=1)))
        return waits

    def whole(part, p):
        return (dkf, dvf)[part][p, 0] + pair_in[part, p].astype(F32)

    settle(0, first_y)
    gradients(0, 0, ZS)
    dq_first = query_start(0)
    settle(1, second_y)
    gradients(1, NEAR, ZS)
    pair_far = pair(NEAR, ZS)
    gradients(1, 3, NEAR)
    pair_mid = pair(3, NEAR)
    step = {}
    for part, way in ((0, 1), (1, -1)):
        pair_far[part]()
        for d in (4, 3, -3):
            red_out[part, POS[d]] = whole(part, POS[d]).astype(BF16)
        step[2, part] = copy(red_out.at[part, POS[4]], red_in.at[2, part], dict(dz=2 * way))
        step[0, part] = copy(red_out.at[part, POS[3]], red_in.at[0, part], dict(dz=1))
        step[1, part] = copy(red_out.at[part, POS[-3]], red_in.at[1, part], dict(dz=-1))
    gradients(1, 0, 3)
    pair_near = pair(0, 3)
    dq_second = query_start(1)
    dq_first = query_second(0, dq_first)
    done(pair_mid)
    done(pair_near)
    for n, d in ((3, 1), (4, -1)):
        for part in range(2):
            red_out[part, POS[d]] = whole(part, POS[d]).astype(BF16)
            step[n, part] = copy(red_out.at[part, POS[d]], red_in.at[n, part], dict(dz=d))
    for part in range(2):
        step[2, part]()
        for n, d in ((0, 2), (1, -2)):
            step[n, part]()
            total = whole(part, POS[d]) + red_in[n, part].astype(F32)
            if n == part:
                total = total + red_in[2, part].astype(F32)
            relay_out[n, part] = total.astype(BF16)
            step[5 + n, part] = copy(relay_out.at[n, part], red_in.at[5 + n, part], dict(dz=d))
    dq_second = query_second(1, dq_second)
    sums = query_sum(0, dq_first) + query_sum(1, dq_second)
    dq_ref[0] = (turned(jnp.concatenate(sums, axis=0), fwd[...], 1) * SCALE).astype(BF16)
    for part, (out, factor) in enumerate(((dk_ref, SCALE), (dv_ref, 1.0))):
        total = whole(part, 0)
        for n in (3, 4, 5, 6):
            step[n, part]()
            total = total + red_in[n, part].astype(F32)
        out[0] = (turned(total, bwd[...], 1) * factor).astype(BF16)
    for src, sem in pending:
        pltpu.make_async_copy(src, src, sem).wait()
    assert taken[0] <= SEMS


def per_device(queries, keys, values, out_grad, poses, pose_index):
    block = jax.ShapeDtypeStruct((1, TOK, HD), BF16)
    vmem = pl.BlockSpec(memory_space=pltpu.VMEM)
    smem = pl.BlockSpec(memory_space=pltpu.SMEM)

    def buf(*shape, kind=BF16):
        return pltpu.VMEM(shape, kind)

    part = HALF // 2
    return pl.pallas_call(
        kernel,
        out_shape=(block, block, block),
        in_specs=[vmem] * 4 + [smem] * 2,
        out_specs=(vmem, vmem, vmem),
        scratch_shapes=[
            buf(2, YS, XS, HALF, HD), buf(2, XS, YS, HALF, HD), buf(ZS, 2, 2, TOK, HD),
            buf(COLS, ROWS, kind=F32), buf(COLS, ROWS, kind=F32),
            buf(2, 2, 8, LANES, kind=F32), buf(2, 2, 8, LANES, kind=F32), buf(2, 2, 8, LANES, kind=F32),
            buf(2, 2, 8, TOK, kind=F32), buf(2, 3, 2, 8, TOK, kind=F32),
            buf(2, 2, 8, TOK, kind=F32), buf(2, 3, 2, 8, TOK, kind=F32),
            buf(2, 2, 8, LANES, kind=F32), buf(2, 1, LANES, kind=F32),
            buf(ZS, 2, TOK, HD, kind=F32), buf(ZS, 2, TOK, HD, kind=F32), buf(2, HD, LANES, kind=F32),
            buf(2, ZS, TOK, HD), buf(2, ZS, TOK, HD),
            buf(2, ZS, TOK, HD), buf(2, 2, TOK, HD), buf(7, 2, TOK, HD),
            buf(2, YS, XS, part, HD), buf(2, 3, XS, part, HD), buf(2, XS, part, HD), buf(2, 3, part, HD),
            buf(2, XS, YS, part, HD), buf(2, 3, YS, part, HD), buf(2, YS, part, HD), buf(2, 3, part, HD),
            buf(HD, HD, kind=F32), buf(HD, HD, kind=F32),
            pltpu.SemaphoreType.DMA((SEMS,)), pltpu.SemaphoreType.DMA((SEMS,)),
        ],
        compiler_params=pltpu.CompilerParams(
            collective_id=0, has_side_effects=True, vmem_limit_bytes=58 * 2**20
        ),
    )(queries, keys, values, out_grad, jnp.transpose(poses, (1, 2, 0)), pose_index)


def solution(mesh):
    block = P("view", "tok", None)
    return jax.shard_map(
        per_device, mesh=mesh, in_specs=(block,) * 4 + (P(), P()), out_specs=(block,) * 3, check_vma=False
    )
```

```python
import math

import jax
import jax.numpy as jnp
from jax import lax
from jax.experimental import pallas as pl
from jax.experimental.pallas import tpu as pltpu
from jax.sharding import PartitionSpec as P

F32 = jnp.float32
BF16 = jnp.bfloat16
MESH = pl.DeviceIdType.MESH
HD = 128
TOK = 128
XS, YS, ZS = 4, 4, 8
ROWS = XS * YS * TOK
COLS = ZS * 2 * TOK
SCALE = HD**-0.5
SCALE2 = SCALE / math.log(2.0)
RECV_SEMS = 55
SEND_SEMS = 4
BUCKET = 2**20
HALF = TOK // 2
LANES = ROWS // 2
DIST = (0, 1, -1, 2, -2, 3, -3, 4)
POS = {d: p for p, d in enumerate(DIST)}
UNROLL = True
NEAR = 5


def nt(a, b):
    return lax.dot_general(a, b, (((1,), (1,)), ((), ())), preferred_element_type=F32)


def nn(a, b):
    return lax.dot_general(a, b, (((1,), (0,)), ((), ())), preferred_element_type=F32)


def turned(a, b, b_dim):
    return lax.dot_general(
        a, b, (((1,), (b_dim,)), ((), ())),
        precision=lax.Precision.HIGHEST, preferred_element_type=F32,
    )


def tables(poses, pose_index, view):
    row = pose_index[view]
    mat = [[poses[i, j, row] for j in range(4)] for i in range(4)]
    back = [[mat[i][j] for j in range(3)] + [mat[3][i]] for i in range(3)]
    back.append(
        [-(mat[0][j] * mat[0][3] + mat[1][j] * mat[1][3] + mat[2][j] * mat[2][3]) for j in range(3)]
        + [mat[3][3]]
    )
    i = lax.broadcasted_iota(jnp.int32, (HD, HD), 0)
    j = lax.broadcasted_iota(jnp.int32, (HD, HD), 1)
    place = jnp.where(i // 4 == j // 4, (i % 4) * 4 + j % 4, 16)
    forward = jnp.zeros((HD, HD), F32)
    backward = jnp.zeros((HD, HD), F32)
    for a in range(4):
        for b in range(4):
            here = place == 4 * a + b
            forward = jnp.where(here, mat[a][b], forward)
            backward = jnp.where(here, back[a][b], backward)
    return forward, backward


def kernel(
    q_ref, k_ref, v_ref, g_ref, poses, pose_index, out_ref,
    qb, gb, kv, wt, sl, pk, ms, mo, st, stx, mid, sty, fs, cs, dkf, dvf, dqt,
    pair_out, pair_in, red_out, relay_out, red_in,
    qa, qa_in, qa_mid, qa_fin, qc, qc_in, qc_mid, qc_fin, fwd, bwd, send_sem, recv_sem,
):
    view = lax.axis_index("view")
    tok = lax.axis_index("tok")
    y = view // 2
    x = (tok // 16) * 2 + view % 2
    z = (tok // 2) % 8
    c = tok % 2
    taken = [0]
    sent = [0]

    def device(dx=0, dy=0, dz=0, dc=0):
        px, py, pz, pc = (x + dx) % XS, (y + dy) % YS, (z + dz + ZS) % ZS, (c + dc) % 2
        return (py * 2 + px % 2, ((px // 2) * ZS + pz) * 2 + pc)

    def amount(ref):
        return math.prod(ref.shape) * jnp.dtype(ref.dtype).itemsize

    def settle_bytes(total, sem):
        rows = total // (4 * HD)
        span = wt.at[:rows, :HD]
        pltpu.make_async_copy(span, span, sem).wait()

    def copies(*sends):
        n = taken[0]
        taken[0] += 1
        total = 0
        for src, dst, to in sends:
            size = amount(src)
            total += size
            if sent[-1] + size > BUCKET:
                sent.append(0)
            sent[-1] += size
            pltpu.make_async_remote_copy(
                src_ref=src, dst_ref=dst, send_sem=send_sem.at[len(sent) - 1], recv_sem=recv_sem.at[n],
                device_id=device(**to), device_id_type=MESH,
            ).start()
        return lambda: settle_bytes(total, recv_sem.at[n])

    def done(*waits):
        for wait in waits:
            wait()

    barrier = pltpu.get_barrier_semaphore()
    peers = [dict(dx=d) for d in (1, 2, 3)] + [dict(dy=d) for d in (1, 2, 3)]
    peers += [dict(dz=d) for d in (1, -1, 2, -2)] + [dict(dc=1)]
    for peer in peers:
        pl.semaphore_signal(barrier, inc=1, device_id=device(**peer), device_id_type=MESH)

    forward, backward = tables(poses, pose_index, view)
    fwd[...] = forward
    bwd[...] = backward
    kv[0, 0, 0] = turned(k_ref[0].astype(F32), backward, 0).astype(BF16)
    kv[0, 0, 1] = turned(v_ref[0].astype(F32), backward, 0).astype(BF16)
    q_own = turned(q_ref[0].astype(F32), forward, 0).astype(BF16)
    g_own = turned(g_ref[0].astype(F32), forward, 0).astype(BF16)
    for h in range(2):
        qb[h, y, x] = q_own[h * HALF : h * HALF + HALF]
        gb[h, x, y] = g_own[h * HALF : h * HALF + HALF]
    dqt[...] = jnp.zeros_like(dqt)
    pl.semaphore_wait(barrier, len(peers))

    def onward(p, part, to_p, distance):
        return (kv.at[p, 0, part], kv.at[to_p, 0, part], dict(dz=distance))

    ahead, behind = [None, None], [None, None]
    ahead[0] = copies(onward(0, 0, POS[-2], 2))
    behind[1] = copies(onward(0, 1, POS[2], -2))
    first, second = [], []
    for h in range(2):
        first.append([
            copies(*[(qb.at[h, y, x], qb.at[h, y, x], dict(dx=d)) for d in (1, 3, 2)]),
            copies(*[(gb.at[h, x, y], gb.at[h, x, y], dict(dy=d)) for d in (1, 3, 2)]),
        ])
        if h == 0:
            ahead[1] = copies(onward(0, 1, POS[-2], 2))
            behind[0] = copies(onward(0, 0, POS[2], -2))
    shared = [copies((kv.at[0, 0], kv.at[0, 1], dict(dc=1)))]
    beside = copies((kv.at[0, 0], kv.at[POS[-1], 0], dict(dz=1)), (kv.at[0, 0], kv.at[POS[1], 0], dict(dz=-1)))

    def share(*pieces):
        return copies(*[(kv.at[p, 0, part], kv.at[p, 1, part], dict(dc=1)) for p, part in pieces])

    for h in range(2):
        first[h][0]()
        q_bundles = [(qb.at[h, y], qb.at[h, y], dict(dy=d)) for d in (1, 3, 2)]
        if h == 0:
            far = {}
            for part, way in ((0, 1), (1, -1)):
                (ahead, behind)[part][part]()
                p = POS[-2 * way]
                far[4, part] = copies(onward(p, part, POS[4], 2 * way))
                far[-3 * way, part] = copies(onward(p, part, POS[-3 * way], way))
                shared.append(share((p, part)))
        first[h][1]()
        g_bundles = [(gb.at[h, x], gb.at[h, x], dict(dx=d)) for d in (1, 3, 2)]
        second.append(copies(*q_bundles, *g_bundles))
    for part, way in ((1, 1), (0, -1)):
        (behind, ahead)[part][part]()
        p = POS[-2 * way]
        far[-3 * way, part] = copies(onward(p, part, POS[-3 * way], way))
        shared.append(share((p, part)))
    beside()
    shared.append(share(*[(POS[d], part) for d in (1, -1) for part in range(2)]))
    done(*shared)

    def scores(h, ch, tiles=range(LANES // TOK)):
        lo, hi = ((0, NEAR), (NEAR, ZS))[ch]
        n = (hi - lo) * 256
        for i in tiles:
            ry, rx = i // 2, (i % 2) * 2
            lanes = slice(h * LANES + i * TOK, h * LANES + i * TOK + TOK)
            here = slice(i * TOK, i * TOK + TOK)
            s = nt(kv[lo:hi, :, 0].reshape(n, HD), qb[h, ry, rx : rx + 2].reshape(TOK, HD)) * SCALE2
            t = nt(kv[lo:hi, :, 1].reshape(n, HD), gb[h, rx : rx + 2, ry].reshape(TOK, HD))
            sl[lo * 256 : hi * 256, lanes] = t
            s = s.reshape(n // 8, 8, TOK)
            peak = jnp.max(s, axis=0)
            w = jnp.exp2(s - peak[None])
            wt[lo * 256 : hi * 256, lanes] = w.reshape(n, TOK)
            pk[h, ch, :, here] = peak
            ms[h, ch, :, here] = jnp.sum(w, axis=0)
            mo[h, ch, :, here] = jnp.sum(w * t.reshape(n // 8, 8, TOK), axis=0)

    def local_statistics(h):
        top = jnp.maximum(pk[h, 0], pk[h, 1])
        row_top = jnp.max(top, axis=0, keepdims=True)
        near, far_off = jnp.exp2(pk[h, 0] - row_top), jnp.exp2(pk[h, 1] - row_top)
        mass = jnp.sum(ms[h, 0] * near + ms[h, 1] * far_off, axis=0, keepdims=True)
        moment = jnp.sum(mo[h, 0] * near + mo[h, 1] * far_off, axis=0, keepdims=True)
        log_mass = row_top + jnp.log2(mass)
        centre = moment / mass
        for i in range(LANES // TOK):
            st[h, 0, i : i + 1, :] = log_mass[:, i * TOK : i * TOK + TOK]
            st[h, 1, i : i + 1, :] = centre[:, i * TOK : i * TOK + TOK]

    def merge(parts):
        logs = [part[0] for part in parts]
        top = logs[0]
        for log in logs[1:]:
            top = jnp.maximum(top, log)
        weights = [jnp.exp2(log - top) for log in logs]
        mass = weights[0]
        moment = weights[0] * parts[0][1]
        for weight, part in zip(weights[1:], parts[1:]):
            mass = mass + weight
            moment = moment + weight * part[1]
        return top + jnp.log2(mass), moment / mass

    def along_x(h):
        return copies(*[(st.at[h], stx.at[h, d - 1], dict(dx=d)) for d in (1, 3, 2)])

    def along_y(h, wait):
        wait()
        log_mass, centre = merge([st.at[h]] + [stx.at[h, d] for d in range(3)])
        mid[h, 0] = log_mass
        mid[h, 1] = centre
        return copies(*[(mid.at[h], sty.at[h, d - 1], dict(dy=d)) for d in (1, 3, 2)])

    def settle(h, wait):
        wait()
        log_mass, centre = merge([mid.at[h]] + [sty.at[h, d] for d in range(3)])
        for i in range(LANES // TOK):
            here = slice(i * TOK, i * TOK + TOK)
            cs[h, :, here] = centre[i : i + 1, :]
            for ch in range(2):
                fs[h, ch, :, here] = jnp.exp2(pk[h, ch, :, here] - log_mass[i : i + 1, :])

    second[0]()
    scores(0, 0, range(0, 4))
    last_shared = []
    for d, part in ((4, 0), (4, 1), (-3, 0), (3, 1), (-3, 1), (3, 0)):
        far[d, part]()
        last_shared.append(share((POS[d], part)))
    scores(0, 0, range(4, 8))
    second[1]()
    scores(1, 0)
    done(*last_shared)
    scores(0, 1)
    local_statistics(0)
    first_x = along_x(0)
    scores(1, 1)
    local_statistics(1)
    second_x = along_x(1)
    first_y = along_y(0, first_x)
    second_y = along_y(1, second_x)

    def gradients(h, lo, hi):
        def block(p, carry):
            ch = p // NEAR
            cols = pl.ds(pl.multiple_of(p * 256, 256), 256)
            kt = kv[p, :, 0].reshape(256, HD).T
            if h == 0:
                dk = jnp.zeros((256, HD), F32)
                dv = jnp.zeros((256, HD), F32)
            else:
                dk = dkf[p].reshape(256, HD)
                dv = dvf[p].reshape(256, HD)
            for ry in range(YS):
                here = slice(ry * 256, ry * 256 + 256)
                lanes = slice(h * LANES + ry * 256, h * LANES + ry * 256 + 256)
                w = wt[cols, lanes].reshape(32, 8, 256)
                probs = (w * fs[h, ch, :, here][None]).reshape(256, 256)
                ds = (probs * (sl[cols, lanes] - cs[h, :, here])).astype(BF16)
                dk = dk + nn(ds, qb[h, ry].reshape(256, HD))
                dv = dv + nn(probs.astype(BF16), gb[h, :, ry].reshape(256, HD))
                dqt[h, :, here] += nn(kt, ds)
            dkf[p] = dk.reshape(2, TOK, HD)
            dvf[p] = dv.reshape(2, TOK, HD)
            return carry

        lax.fori_loop(lo, hi, block, 0, unroll=UNROLL)

    def query_start(h):
        for i in range(LANES // TOK):
            rows = dqt[h, :, i * TOK : i * TOK + TOK].T.astype(BF16)
            for b in range(2):
                ry, rx = i // 2, (i % 2) * 2 + b
                qa[h, ry, rx] = rows[b * HALF : b * HALF + HALF // 2]
                qc[h, rx, ry] = rows[b * HALF + HALF // 2 : b * HALF + HALF]
        a = copies(*[(qa.at[h, (y + d) % YS], qa_in.at[h, d - 1], dict(dy=d)) for d in (1, 3, 2)])
        b = copies(*[(qc.at[h, (x + d) % XS], qc_in.at[h, d - 1], dict(dx=d)) for d in (1, 3, 2)])
        return a, b

    def four(mine, others):
        total = mine.astype(F32)
        for n in range(3):
            total = total + others[n].astype(F32)
        return total

    def query_second(h, waits):
        waits[0]()
        qa_mid[h] = four(qa[h, y], qa_in[h]).astype(BF16)
        a = copies(*[(qa_mid.at[h, (x + d) % XS], qa_fin.at[h, d - 1], dict(dx=d)) for d in (1, 3, 2)])
        waits[1]()
        qc_mid[h] = four(qc[h, x], qc_in[h]).astype(BF16)
        b = copies(*[(qc_mid.at[h, (y + d) % YS], qc_fin.at[h, d - 1], dict(dy=d)) for d in (1, 3, 2)])
        return a, b

    def query_sum(h, waits):
        done(*waits)
        return [four(qa_mid[h, x], qa_fin[h]), four(qc_mid[h, y], qc_fin[h])]

    def pair(lo, hi):
        sends = []
        for part, total in enumerate((dkf, dvf)):
            pair_out[part, lo:hi] = total[lo:hi, 1].astype(BF16)
            sends.append((pair_out.at[part, lo:hi], pair_in.at[part, lo:hi], dict(dc=1)))
        return copies(*sends)

    def whole(part, p):
        return (dkf, dvf)[part][p, 0] + pair_in[part, p].astype(F32)

    settle(0, first_y)
    gradients(0, NEAR, ZS)
    settle(1, second_y)
    gradients(1, NEAR, ZS)
    pair_far = pair(NEAR, ZS)
    gradients(0, 0, 3)
    pair_far()
    step = {}
    for part, way in ((0, 1), (1, -1)):
        for d in (4, 3, -3):
            red_out[part, POS[d]] = whole(part, POS[d]).astype(BF16)
        step[2, part] = copies((red_out.at[part, POS[4]], red_in.at[2, part], dict(dz=2 * way)))
        step[0, part] = copies((red_out.at[part, POS[3]], red_in.at[0, part], dict(dz=1)))
        step[1, part] = copies((red_out.at[part, POS[-3]], red_in.at[1, part], dict(dz=-1)))
    gradients(1, 0, 3)
    pair_near = pair(0, 3)
    gradients(0, 3, NEAR)
    pair_near()
    sends = []
    for n, d in ((3, 1), (4, -1)):
        for part in range(2):
            red_out[part, POS[d]] = whole(part, POS[d]).astype(BF16)
            sends.append((red_out.at[part, POS[d]], red_in.at[n, part], dict(dz=d)))
    direct = copies(*sends)
    dq_first = query_start(0)
    gradients(1, 3, NEAR)
    pair_mid = pair(3, NEAR)
    dq_second = query_start(1)
    dq_first = query_second(0, dq_first)
    pair_mid()
    relayed = []
    for n, part in ((1, 0), (0, 0), (1, 1), (0, 1)):
        d = (2, -2)[n]
        step[n, part]()
        total = whole(part, POS[d]) + red_in[n, part].astype(F32)
        if n == part:
            step[2, part]()
            total = total + red_in[2, part].astype(F32)
        relay_out[n, part] = total.astype(BF16)
        relayed.append(copies((relay_out.at[n, part], red_in.at[5 + n, part], dict(dz=d))))
    dq_second = query_second(1, dq_second)
    sums = query_sum(0, dq_first) + query_sum(1, dq_second)
    out_ref[0] = (turned(jnp.concatenate(sums, axis=0), fwd[...], 1) * SCALE).astype(BF16)
    direct()
    done(*relayed)
    for part, factor in enumerate((SCALE, 1.0)):
        total = whole(part, 0)
        for n in (3, 4, 5, 6):
            total = total + red_in[n, part].astype(F32)
        out_ref[1 + part] = (turned(total, bwd[...], 1) * factor).astype(BF16)
    for n, total in enumerate(sent):
        settle_bytes(total, send_sem.at[n])
    assert taken[0] <= RECV_SEMS and len(sent) <= SEND_SEMS


def per_device(queries, keys, values, out_grad, poses, pose_index):
    vmem = pl.BlockSpec(memory_space=pltpu.VMEM)
    smem = pl.BlockSpec(memory_space=pltpu.SMEM)

    def buf(*shape, kind=BF16):
        return pltpu.VMEM(shape, kind)

    part = HALF // 2
    out = pl.pallas_call(
        kernel,
        out_shape=jax.ShapeDtypeStruct((3, TOK, HD), BF16),
        in_specs=[vmem] * 4 + [smem] * 2,
        out_specs=vmem,
        scratch_shapes=[
            buf(2, YS, XS, HALF, HD), buf(2, XS, YS, HALF, HD), buf(ZS, 2, 2, TOK, HD),
            buf(COLS, ROWS, kind=F32), buf(COLS, ROWS, kind=F32),
            buf(2, 2, 8, LANES, kind=F32), buf(2, 2, 8, LANES, kind=F32), buf(2, 2, 8, LANES, kind=F32),
            buf(2, 2, 8, TOK, kind=F32), buf(2, 3, 2, 8, TOK, kind=F32),
            buf(2, 2, 8, TOK, kind=F32), buf(2, 3, 2, 8, TOK, kind=F32),
            buf(2, 2, 8, LANES, kind=F32), buf(2, 1, LANES, kind=F32),
            buf(ZS, 2, TOK, HD, kind=F32), buf(ZS, 2, TOK, HD, kind=F32), buf(2, HD, LANES, kind=F32),
            buf(2, ZS, TOK, HD), buf(2, ZS, TOK, HD),
            buf(2, ZS, TOK, HD), buf(2, 2, TOK, HD), buf(7, 2, TOK, HD),
            buf(2, YS, XS, part, HD), buf(2, 3, XS, part, HD), buf(2, XS, part, HD), buf(2, 3, part, HD),
            buf(2, XS, YS, part, HD), buf(2, 3, YS, part, HD), buf(2, YS, part, HD), buf(2, 3, part, HD),
            buf(HD, HD, kind=F32), buf(HD, HD, kind=F32),
            pltpu.SemaphoreType.DMA((SEND_SEMS,)), pltpu.SemaphoreType.DMA((RECV_SEMS,)),
        ],
        compiler_params=pltpu.CompilerParams(
            collective_id=0, has_side_effects=True, vmem_limit_bytes=58 * 2**20
        ),
    )(queries, keys, values, out_grad, jnp.transpose(poses, (1, 2, 0)), pose_index)
    return out[0:1], out[1:2], out[2:3]


def solution(mesh):
    block = P("view", "tok", None)
    return jax.shard_map(
        per_device, mesh=mesh, in_specs=(block,) * 4 + (P(), P()), out_specs=(block,) * 3, check_vma=False
    )
```

```python
import math

import jax
import jax.numpy as jnp
from jax import lax
from jax.experimental import pallas as pl
from jax.experimental.pallas import tpu as pltpu
from jax.sharding import PartitionSpec as P

F32 = jnp.float32
BF16 = jnp.bfloat16
MESH = pl.DeviceIdType.MESH
HD = 128
TOK = 128
XS, YS, ZS = 4, 4, 8
ROWS = XS * YS * TOK
COLS = ZS * 2 * TOK
SCALE = HD**-0.5
SCALE2 = SCALE / math.log(2.0)
RECV_SEMS = 46
SEND_SEMS = 4
BUCKET = 2**20
HALF = TOK // 2
LANES = ROWS // 2
TILES = ROWS // TOK
DIST = (0, 1, -1, 2, -2, 3, -3, 4)
POS = {d: p for p, d in enumerate(DIST)}
NEAR = 5


def nt(a, b):
    return lax.dot_general(a, b, (((1,), (1,)), ((), ())), preferred_element_type=F32)


def nn(a, b):
    return lax.dot_general(a, b, (((1,), (0,)), ((), ())), preferred_element_type=F32)


def turned(a, b, b_dim):
    return lax.dot_general(
        a, b, (((1,), (b_dim,)), ((), ())),
        precision=lax.Precision.HIGHEST, preferred_element_type=F32,
    )


def tables(poses, pose_index, view):
    row = pose_index[view]
    mat = [[poses[i, j, row] for j in range(4)] for i in range(4)]
    back = [[mat[i][j] for j in range(3)] + [mat[3][i]] for i in range(3)]
    back.append(
        [-(mat[0][j] * mat[0][3] + mat[1][j] * mat[1][3] + mat[2][j] * mat[2][3]) for j in range(3)]
        + [mat[3][3]]
    )
    i = lax.broadcasted_iota(jnp.int32, (HD, HD), 0)
    j = lax.broadcasted_iota(jnp.int32, (HD, HD), 1)
    place = jnp.where(i // 4 == j // 4, (i % 4) * 4 + j % 4, 16)
    forward = jnp.zeros((HD, HD), F32)
    backward = jnp.zeros((HD, HD), F32)
    for a in range(4):
        for b in range(4):
            here = place == 4 * a + b
            forward = jnp.where(here, mat[a][b], forward)
            backward = jnp.where(here, back[a][b], backward)
    return forward, backward


def kernel(
    q_ref, k_ref, v_ref, g_ref, poses, pose_index, out_ref,
    qb, gb, kv, wt, sl, pk, ms, mo, st, stx, mid, sty, share_x, share_y, fs, cs, dst, dkf, dvf, dqt,
    pair_out, pair_in, red_out, relay_out, red_in,
    qa, qa_in, qa_mid, qa_fin, qc, qc_in, qc_mid, qc_fin, fwd, bwd, send_sem, recv_sem,
):
    view = lax.axis_index("view")
    tok = lax.axis_index("tok")
    y = view // 2
    x = (tok // 16) * 2 + view % 2
    z = (tok // 2) % 8
    c = tok % 2
    taken = [0]
    sent = [0]
    ring = (1, 3, 2)

    def device(dx=0, dy=0, dz=0, dc=0):
        px, py, pz, pc = (x + dx) % XS, (y + dy) % YS, (z + dz + ZS) % ZS, (c + dc) % 2
        return (py * 2 + px % 2, ((px // 2) * ZS + pz) * 2 + pc)

    def amount(ref):
        return math.prod(ref.shape) * jnp.dtype(ref.dtype).itemsize

    def settle_bytes(total, sem):
        rows = total // (4 * HD)
        span = wt.at[:rows, :HD]
        pltpu.make_async_copy(span, span, sem).wait()

    class Group:
        def __init__(self, *sends):
            self.n = taken[0]
            self.total = 0
            taken[0] += 1
            self.add(*sends)

        def add(self, *sends):
            for src, dst, to in sends:
                size = amount(src)
                self.total += size
                if sent[-1] + size > BUCKET:
                    sent.append(0)
                sent[-1] += size
                pltpu.make_async_remote_copy(
                    src_ref=src, dst_ref=dst, send_sem=send_sem.at[len(sent) - 1], recv_sem=recv_sem.at[self.n],
                    device_id=device(**to), device_id_type=MESH,
                ).start()

        def wait(self):
            settle_bytes(self.total, recv_sem.at[self.n])

    barrier = pltpu.get_barrier_semaphore()
    peers = [dict(dx=d) for d in ring] + [dict(dy=d) for d in ring]
    peers += [dict(dz=d) for d in (1, -1, 2, -2)] + [dict(dc=1)]
    for peer in peers:
        pl.semaphore_signal(barrier, inc=1, device_id=device(**peer), device_id_type=MESH)

    forward, backward = tables(poses, pose_index, view)
    fwd[...] = forward
    bwd[...] = backward
    for ref, buf in ((q_ref, qb), (g_ref, gb)):
        own = turned(ref[0].astype(F32), forward, 0).astype(BF16)
        buf[0, y, x] = own[:HALF]
        buf[1, x, y] = own[HALF:]
    kv[0, 0, 0] = turned(k_ref[0].astype(F32), backward, 0).astype(BF16)
    kv[0, 0, 1] = turned(v_ref[0].astype(F32), backward, 0).astype(BF16)
    dqt[...] = jnp.zeros_like(dqt)
    pl.semaphore_wait(barrier, len(peers))

    def rows_first(buf):
        return (
            Group(*[(buf.at[0, y, x], buf.at[0, y, x], dict(dx=d)) for d in ring]),
            Group(*[(buf.at[1, x, y], buf.at[1, x, y], dict(dy=d)) for d in ring]),
        )

    def rows_second(buf, first):
        first[0].wait()
        group = Group(*[(buf.at[0, y], buf.at[0, y], dict(dy=d)) for d in ring])
        first[1].wait()
        group.add(*[(buf.at[1, x], buf.at[1, x], dict(dx=d)) for d in ring])
        return group

    def onward(part, p, to_p, distance, span=slice(None)):
        return (kv.at[p, 0, part, span], kv.at[to_p, 0, part, span], dict(dz=distance))

    def across(part, *places):
        return [(kv.at[p, 0, part], kv.at[p, 1, part], dict(dc=1)) for p in places]

    def columns_first(part):
        ahead = Group(onward(part, 0, POS[-2], 2))
        behind = Group(onward(part, 0, POS[2], -2))
        beside = Group(onward(part, 0, POS[-1], 1), onward(part, 0, POS[1], -1))
        return ahead, behind, beside

    def columns_second(part, first, near):
        far = None
        for way, span in ((1, slice(0, HALF)), (-1, slice(HALF, TOK))):
            first[0 if way == 1 else 1].wait()
            p = POS[-2 * way]
            sends = (onward(part, p, POS[4], 2 * way, span), onward(part, p, POS[-3 * way], way))
            if far is None:
                far = Group(*sends)
            else:
                far.add(*sends)
            near.add(*across(part, p))
        first[2].wait()
        near.add(*across(part, POS[1], POS[-1]))
        return far

    keys_first = columns_first(0)
    q_first = rows_first(qb)
    keys_near = Group(*across(0, 0))
    values_first = columns_first(1)
    g_first = rows_first(gb)
    values_near = Group(*across(1, 0))
    q_second = rows_second(qb, q_first)
    keys_far = columns_second(0, keys_first, keys_near)
    g_second = rows_second(gb, g_first)
    values_far = columns_second(1, values_first, values_near)

    def tile(buf, i):
        h, i = i // 8, i % 8
        ry, rx = i // 2, (i % 2) * 2
        part = buf[0, ry, rx : rx + 2] if h == 0 else buf[1, rx : rx + 2, ry]
        return part.reshape(TOK, HD)

    def wide(buf, i):
        return (buf[0, i] if i < YS else buf[1, :, i - YS]).reshape(2 * TOK, HD)

    def bounds(ch):
        lo, hi = ((0, NEAR), (NEAR, ZS))[ch]
        return lo, hi, slice(lo * 256, hi * 256), (hi - lo) * 256

    def scores(ch, tiles=range(TILES)):
        lo, hi, cols, n = bounds(ch)
        for i in tiles:
            lanes = slice(i * TOK, i * TOK + TOK)
            s = nt(kv[lo:hi, :, 0].reshape(n, HD), tile(qb, i)) * SCALE2
            s = s.reshape(hi - lo, 32, 8, TOK)
            peak = jnp.max(s, axis=1)
            w = jnp.exp2(s - peak[:, None])
            wt[cols, lanes] = w.reshape(n, TOK)
            pk[lo:hi, :, lanes] = peak
            ms[lo:hi, :, lanes] = jnp.sum(w, axis=1)

    def slopes(ch, tiles=range(TILES)):
        lo, hi, cols, n = bounds(ch)
        for i in tiles:
            lanes = slice(i * TOK, i * TOK + TOK)
            t = nt(kv[lo:hi, :, 1].reshape(n, HD), tile(gb, i))
            sl[cols, lanes] = t
            w = wt[cols, lanes].reshape(hi - lo, 32, 8, TOK)
            mo[lo:hi, :, lanes] = jnp.sum(w * t.reshape(hi - lo, 32, 8, TOK), axis=1)

    def local_mass():
        for i in range(TILES):
            lanes = slice(i * TOK, i * TOK + TOK)
            peak = pk[:, :, lanes]
            top = jnp.max(jnp.max(peak, axis=0), axis=0, keepdims=True)
            mass = jnp.sum(jnp.sum(ms[:, :, lanes] * jnp.exp2(peak - top[None]), axis=0), axis=0, keepdims=True)
            log_mass = top + jnp.log2(mass)
            cs[:, lanes] = log_mass
            st[0, i : i + 1, :] = log_mass

    def local_centre():
        for i in range(TILES):
            lanes = slice(i * TOK, i * TOK + TOK)
            factor = jnp.exp2(pk[:, :, lanes] - cs[:, lanes][None])
            st[1, i : i + 1, :] = jnp.sum(jnp.sum(mo[:, :, lanes] * factor, axis=0), axis=0, keepdims=True)

    def spread(src, landing, n, axis):
        return Group(*[(src.at[n], landing.at[n, d - 1], {axis: d}) for d in ring])

    def merge_mass(mine, landing, shares):
        logs = [mine[0]] + [landing[0, n] for n in range(3)]
        top = jnp.maximum(jnp.maximum(logs[0], logs[1]), jnp.maximum(logs[2], logs[3]))
        weights = [jnp.exp2(log - top) for log in logs]
        mass = weights[0] + weights[1] + weights[2] + weights[3]
        for n in range(4):
            shares[n] = weights[n] / mass
        return top + jnp.log2(mass)

    def merge_centre(mine, landing, shares):
        total = mine[1] * shares[0]
        for n in range(3):
            total = total + landing[1, n] * shares[n + 1]
        return total

    q_second.wait()
    keys_near.wait()
    scores(0, range(0, 8))
    keys_far.wait()
    keys_last = Group(*across(0, POS[4], POS[3], POS[-3]))
    scores(0, range(8, TILES))
    keys_last.wait()
    scores(1)
    local_mass()
    mass_x = spread(st, stx, 0, "dx")
    values_far.wait()
    values_last = Group(*across(1, POS[4], POS[3], POS[-3]))
    g_second.wait()
    values_near.wait()
    slopes(0)
    mass_x.wait()
    mid[0] = merge_mass(st, stx, share_x)
    mass_y = spread(mid, sty, 0, "dy")
    values_last.wait()
    slopes(1)
    local_centre()
    centre_x = spread(st, stx, 1, "dx")
    mass_y.wait()
    log_mass = merge_mass(mid, sty, share_y)
    for i in range(TILES):
        lanes = slice(i * TOK, i * TOK + TOK)
        fs[:, :, lanes] = jnp.exp2(pk[:, :, lanes] - log_mass[i : i + 1, :][None])

    def probabilities(p, cols, here):
        w = wt[cols, here].reshape(32, 8, 256)
        return (w * fs[p, :, here][None]).reshape(256, 256)

    def value_gradients(lo, hi):
        for p in range(lo, hi):
            dv = jnp.zeros((256, HD), F32)
            for i in range(ROWS // 256):
                here = slice(i * 256, i * 256 + 256)
                probs = probabilities(p, slice(p * 256, p * 256 + 256), here)
                dv = dv + nn(probs.astype(BF16), wide(gb, i))
            dvf[p] = dv.reshape(2, TOK, HD)

    def slope_gradients(p, kt, i):
        cols = slice(p * 256, p * 256 + 256)
        here = slice(i * 256, i * 256 + 256)
        ds = (probabilities(p, cols, here) * (sl[cols, here] - cs[:, here])).astype(BF16)
        dqt[:, here] += nn(kt, ds)
        return ds

    def key_gradients(lo, hi):
        for p in range(lo, hi):
            kt = kv[p, :, 0].reshape(256, HD).T
            dk = jnp.zeros((256, HD), F32)
            for i in range(ROWS // 256):
                dk = dk + nn(slope_gradients(p, kt, i), wide(qb, i))
            dkf[p] = dk.reshape(2, TOK, HD)

    def query_part(lo, hi, tiles):
        for p in range(lo, hi):
            kt = kv[p, :, 0].reshape(256, HD).T
            for i in tiles:
                dst[p * 256 : p * 256 + 256, i * 256 : i * 256 + 256] = slope_gradients(p, kt, i)

    def key_part(lo, hi):
        for p in range(lo, hi):
            dk = jnp.zeros((256, HD), F32)
            for i in range(ROWS // 256):
                dk = dk + nn(dst[p * 256 : p * 256 + 256, i * 256 : i * 256 + 256], wide(qb, i))
            dkf[p] = dk.reshape(2, TOK, HD)

    totals = (dkf, dvf)

    def pair(part, lo, hi):
        pair_out[part, lo:hi] = totals[part][lo:hi, 1].astype(BF16)
        return Group((pair_out.at[part, lo:hi], pair_in.at[part, lo:hi], dict(dc=1)))

    def whole(part, p):
        return totals[part][p, 0] + pair_in[part, p].astype(F32)

    def outward(part):
        for d in (4, 3, -3):
            red_out[part, POS[d]] = whole(part, POS[d]).astype(BF16)
        waits = []
        for n, way, span in ((0, 1, slice(0, HALF)), (1, -1, slice(HALF, TOK))):
            waits.append(Group(
                (red_out.at[part, POS[4], span], red_in.at[2, part, span], dict(dz=2 * way)),
                (red_out.at[part, POS[3 * way]], red_in.at[n, part], dict(dz=way)),
            ))
        return waits

    def direct(part):
        for d in (1, -1):
            red_out[part, POS[d]] = whole(part, POS[d]).astype(BF16)
        return Group(*[
            (red_out.at[part, POS[d]], red_in.at[n, part], dict(dz=d)) for n, d in ((3, 1), (4, -1))
        ])

    def relay(part, waits, group):
        for n, d, span in ((0, 2, slice(0, HALF)), (1, -2, slice(HALF, TOK))):
            waits[n].wait()
            rest = slice(HALF, TOK) if n == 0 else slice(0, HALF)
            total = whole(part, POS[d]) + red_in[n, part].astype(F32)
            relay_out[n, part, span] = (total[span] + red_in[2, part, span].astype(F32)).astype(BF16)
            relay_out[n, part, rest] = total[rest].astype(BF16)
            group.add((relay_out.at[n, part], red_in.at[5 + n, part], dict(dz=d)))

    def owned(part):
        total = whole(part, 0)
        for n in (3, 4, 5, 6):
            total = total + red_in[n, part].astype(F32)
        return total

    def query_start(h):
        for j in range(TILES // 2):
            i = h * (TILES // 2) + j
            rows = dqt[:, i * TOK : i * TOK + TOK].T.astype(BF16)
            for b in range(2):
                ry, rx = j // 2, (j % 2) * 2 + b
                qa[h, ry, rx] = rows[b * HALF : b * HALF + HALF // 2]
                qc[h, rx, ry] = rows[b * HALF + HALF // 2 : b * HALF + HALF]
        return (
            Group(*[(qa.at[h, (y + d) % YS], qa_in.at[h, d - 1], dict(dy=d)) for d in ring]),
            Group(*[(qc.at[h, (x + d) % XS], qc_in.at[h, d - 1], dict(dx=d)) for d in ring]),
        )

    def four(mine, others):
        total = mine.astype(F32)
        for n in range(3):
            total = total + others[n].astype(F32)
        return total

    def query_second(h, waits):
        waits[0].wait()
        qa_mid[h] = four(qa[h, y], qa_in[h]).astype(BF16)
        group = Group(*[(qa_mid.at[h, (x + d) % XS], qa_fin.at[h, d - 1], dict(dx=d)) for d in ring])
        waits[1].wait()
        qc_mid[h] = four(qc[h, x], qc_in[h]).astype(BF16)
        group.add(*[(qc_mid.at[h, (y + d) % YS], qc_fin.at[h, d - 1], dict(dy=d)) for d in ring])
        return group

    def query_sum(h):
        return [four(qa_mid[h, x], qa_fin[h]), four(qc_mid[h, y], qc_fin[h])]

    value_gradients(NEAR, ZS)
    pair_far = pair(1, NEAR, ZS)
    centre_x.wait()
    mid[1] = merge_centre(st, stx, share_x)
    centre_y = spread(mid, sty, 1, "dy")
    value_gradients(0, 3)
    pair_near = pair(1, 0, 3)
    pair_far.wait()
    values_out = outward(1)
    value_gradients(3, NEAR)
    pair_mid = pair(1, 3, NEAR)
    pair_near.wait()
    values_in = direct(1)
    centre_y.wait()
    centre = merge_centre(mid, sty, share_y)
    for i in range(TILES):
        cs[:, i * TOK : i * TOK + TOK] = centre[i : i + 1, :]
    key_gradients(NEAR, ZS)
    pair_far = pair(0, NEAR, ZS)
    query_part(0, NEAR, range(0, YS))
    queries_out = [query_start(0)]
    pair_far.wait()
    keys_out = outward(0)
    query_part(0, NEAR, range(YS, 2 * YS))
    queries_out.append(query_start(1))
    pair_mid.wait()
    relay(1, values_out, values_in)
    key_part(0, 3)
    pair_near = pair(0, 0, 3)
    key_part(3, NEAR)
    pair_mid = pair(0, 3, NEAR)
    pair_near.wait()
    keys_in = direct(0)
    pair_mid.wait()
    queries_in = [query_second(0, queries_out[0])]
    relay(0, keys_out, keys_in)
    queries_in.append(query_second(1, queries_out[1]))
    values_in.wait()
    out_ref[2] = turned(owned(1), bwd[...], 1).astype(BF16)
    queries_in[0].wait()
    queries_in[1].wait()
    dq = jnp.concatenate(query_sum(0) + query_sum(1), axis=0)
    out_ref[0] = (turned(dq, fwd[...], 1) * SCALE).astype(BF16)
    keys_in.wait()
    out_ref[1] = (turned(owned(0), bwd[...], 1) * SCALE).astype(BF16)
    for n, total in enumerate(sent):
        settle_bytes(total, send_sem.at[n])
    assert taken[0] <= RECV_SEMS and len(sent) <= SEND_SEMS


def per_device(queries, keys, values, out_grad, poses, pose_index):
    vmem = pl.BlockSpec(memory_space=pltpu.VMEM)
    smem = pl.BlockSpec(memory_space=pltpu.SMEM)

    def buf(*shape, kind=BF16):
        return pltpu.VMEM(shape, kind)

    part = HALF // 2
    out = pl.pallas_call(
        kernel,
        out_shape=jax.ShapeDtypeStruct((3, TOK, HD), BF16),
        in_specs=[vmem] * 4 + [smem] * 2,
        out_specs=vmem,
        scratch_shapes=[
            buf(2, YS, XS, HALF, HD), buf(2, XS, YS, HALF, HD), buf(ZS, 2, 2, TOK, HD),
            buf(COLS, ROWS, kind=F32), buf(COLS, ROWS, kind=F32),
            *[buf(ZS, 8, ROWS, kind=F32)] * 3,
            buf(2, TILES, TOK, kind=F32), buf(2, 3, TILES, TOK, kind=F32),
            buf(2, TILES, TOK, kind=F32), buf(2, 3, TILES, TOK, kind=F32),
            buf(4, TILES, TOK, kind=F32), buf(4, TILES, TOK, kind=F32),
            buf(ZS, 8, ROWS, kind=F32), buf(1, ROWS, kind=F32), buf(NEAR * 256, ROWS),
            buf(ZS, 2, TOK, HD, kind=F32), buf(ZS, 2, TOK, HD, kind=F32), buf(HD, ROWS, kind=F32),
            buf(2, ZS, TOK, HD), buf(2, ZS, TOK, HD),
            buf(2, ZS, TOK, HD), buf(2, 2, TOK, HD), buf(7, 2, TOK, HD),
            buf(2, YS, XS, part, HD), buf(2, 3, XS, part, HD), buf(2, XS, part, HD), buf(2, 3, part, HD),
            buf(2, XS, YS, part, HD), buf(2, 3, YS, part, HD), buf(2, YS, part, HD), buf(2, 3, part, HD),
            buf(HD, HD, kind=F32), buf(HD, HD, kind=F32),
            pltpu.SemaphoreType.DMA((SEND_SEMS,)), pltpu.SemaphoreType.DMA((RECV_SEMS,)),
        ],
        compiler_params=pltpu.CompilerParams(
            collective_id=0, has_side_effects=True, vmem_limit_bytes=58 * 2**20
        ),
    )(queries, keys, values, out_grad, jnp.transpose(poses, (1, 2, 0)), pose_index)
    return out[0:1], out[1:2], out[2:3]


def solution(mesh):
    block = P("view", "tok", None)
    return jax.shard_map(
        per_device, mesh=mesh, in_specs=(block,) * 4 + (P(), P()), out_specs=(block,) * 3, check_vma=False
    )
```

```python
import math

import jax
import jax.numpy as jnp
from jax import lax
from jax.experimental import pallas as pl
from jax.experimental.pallas import tpu as pltpu
from jax.sharding import PartitionSpec as P

F32 = jnp.float32
BF16 = jnp.bfloat16
MESH = pl.DeviceIdType.MESH
HD = 128
TOK = 128
XS, YS, ZS = 4, 4, 8
ROWS = XS * YS * TOK
COLS = ZS * 2 * TOK
SCALE = HD**-0.5
SCALE2 = SCALE / math.log(2.0)
RECV_SEMS = 46
SEND_SEMS = 4
BUCKET = 2**20
HALF = TOK // 2
LANES = ROWS // 2
TILES = ROWS // TOK
DIST = (0, 1, -1, 2, -2, 3, -3, 4)
POS = {d: p for p, d in enumerate(DIST)}
NEAR = 5


def nt(a, b):
    return lax.dot_general(a, b, (((1,), (1,)), ((), ())), preferred_element_type=F32)


def nn(a, b):
    return lax.dot_general(a, b, (((1,), (0,)), ((), ())), preferred_element_type=F32)


def turned(a, b, b_dim):
    return lax.dot_general(
        a, b, (((1,), (b_dim,)), ((), ())),
        precision=lax.Precision.HIGHEST, preferred_element_type=F32,
    )


def tables(poses, pose_index, view):
    row = pose_index[view]
    mat = [[poses[i, j, row] for j in range(4)] for i in range(4)]
    back = [[mat[i][j] for j in range(3)] + [mat[3][i]] for i in range(3)]
    back.append(
        [-(mat[0][j] * mat[0][3] + mat[1][j] * mat[1][3] + mat[2][j] * mat[2][3]) for j in range(3)]
        + [mat[3][3]]
    )
    i = lax.broadcasted_iota(jnp.int32, (HD, HD), 0)
    j = lax.broadcasted_iota(jnp.int32, (HD, HD), 1)
    place = jnp.where(i // 4 == j // 4, (i % 4) * 4 + j % 4, 16)
    forward = jnp.zeros((HD, HD), F32)
    backward = jnp.zeros((HD, HD), F32)
    for a in range(4):
        for b in range(4):
            here = place == 4 * a + b
            forward = jnp.where(here, mat[a][b], forward)
            backward = jnp.where(here, back[a][b], backward)
    return forward, backward


def kernel(
    q_ref, k_ref, v_ref, g_ref, poses, pose_index, out_ref,
    qb, gb, kv, wt, sl, pk, ms, mo, st, stx, mid, sty, share_x, share_y, fs, cs, dst, dkf, dvf, dqt,
    pair_out, pair_in, red_out, relay_out, red_in,
    qa, qa_in, qa_mid, qa_fin, qc, qc_in, qc_mid, qc_fin, fwd, bwd, send_sem, recv_sem,
):
    view = lax.axis_index("view")
    tok = lax.axis_index("tok")
    y = view // 2
    x = (tok // 16) * 2 + view % 2
    z = (tok // 2) % 8
    c = tok % 2
    taken = [0]
    sent = [0]
    ring = (1, 3, 2)

    def device(dx=0, dy=0, dz=0, dc=0):
        px, py, pz, pc = (x + dx) % XS, (y + dy) % YS, (z + dz + ZS) % ZS, (c + dc) % 2
        return (py * 2 + px % 2, ((px // 2) * ZS + pz) * 2 + pc)

    def amount(ref):
        return math.prod(ref.shape) * jnp.dtype(ref.dtype).itemsize

    def settle_bytes(total, sem):
        rows = total // (4 * HD)
        span = wt.at[:rows, :HD]
        pltpu.make_async_copy(span, span, sem).wait()

    class Group:
        def __init__(self, *sends):
            self.n = taken[0]
            self.total = 0
            taken[0] += 1
            self.add(*sends)

        def add(self, *sends):
            for src, dst, to in sends:
                size = amount(src)
                self.total += size
                if sent[-1] + size > BUCKET:
                    sent.append(0)
                sent[-1] += size
                pltpu.make_async_remote_copy(
                    src_ref=src, dst_ref=dst, send_sem=send_sem.at[len(sent) - 1], recv_sem=recv_sem.at[self.n],
                    device_id=device(**to), device_id_type=MESH,
                ).start()

        def wait(self):
            settle_bytes(self.total, recv_sem.at[self.n])

    barrier = pltpu.get_barrier_semaphore()
    peers = [dict(dx=d) for d in ring] + [dict(dy=d) for d in ring]
    peers += [dict(dz=d) for d in (1, -1, 2, -2)] + [dict(dc=1)]
    for peer in peers:
        pl.semaphore_signal(barrier, inc=1, device_id=device(**peer), device_id_type=MESH)

    forward, backward = tables(poses, pose_index, view)
    fwd[...] = forward
    bwd[...] = backward
    for ref, buf in ((q_ref, qb), (g_ref, gb)):
        own = turned(ref[0].astype(F32), forward, 0).astype(BF16)
        buf[0, y, x] = own[:HALF]
        buf[1, x, y] = own[HALF:]
    kv[0, 0, 0] = turned(k_ref[0].astype(F32), backward, 0).astype(BF16)
    kv[0, 0, 1] = turned(v_ref[0].astype(F32), backward, 0).astype(BF16)
    dqt[...] = jnp.zeros_like(dqt)
    pl.semaphore_wait(barrier, len(peers))

    def rows_first(buf):
        return (
            Group(*[(buf.at[0, y, x], buf.at[0, y, x], dict(dx=d)) for d in ring]),
            Group(*[(buf.at[1, x, y], buf.at[1, x, y], dict(dy=d)) for d in ring]),
        )

    def rows_second(buf, first):
        first[0].wait()
        group = Group(*[(buf.at[0, y], buf.at[0, y], dict(dy=d)) for d in ring])
        first[1].wait()
        group.add(*[(buf.at[1, x], buf.at[1, x], dict(dx=d)) for d in ring])
        return group

    def onward(part, p, to_p, distance, span=slice(None)):
        return (kv.at[p, 0, part, span], kv.at[to_p, 0, part, span], dict(dz=distance))

    def across(part, *places):
        return [(kv.at[p, 0, part], kv.at[p, 1, part], dict(dc=1)) for p in places]

    def columns_first(part):
        ahead = Group(onward(part, 0, POS[-2], 2))
        behind = Group(onward(part, 0, POS[2], -2))
        beside = Group(onward(part, 0, POS[-1], 1), onward(part, 0, POS[1], -1))
        return ahead, behind, beside

    def columns_second(part, first, near):
        far = None
        for way, span in ((1, slice(0, HALF)), (-1, slice(HALF, TOK))):
            first[0 if way == 1 else 1].wait()
            p = POS[-2 * way]
            sends = (onward(part, p, POS[4], 2 * way, span), onward(part, p, POS[-3 * way], way))
            if far is None:
                far = Group(*sends)
            else:
                far.add(*sends)
            near.add(*across(part, p))
        first[2].wait()
        near.add(*across(part, POS[1], POS[-1]))
        return far

    keys_first = columns_first(0)
    q_first = rows_first(qb)
    keys_near = Group(*across(0, 0))
    values_first = columns_first(1)
    g_first = rows_first(gb)
    values_near = Group(*across(1, 0))
    q_second = rows_second(qb, q_first)
    keys_far = columns_second(0, keys_first, keys_near)
    g_second = rows_second(gb, g_first)
    values_far = columns_second(1, values_first, values_near)

    def tile(buf, i):
        h, i = i // 8, i % 8
        ry, rx = i // 2, (i % 2) * 2
        part = buf[0, ry, rx : rx + 2] if h == 0 else buf[1, rx : rx + 2, ry]
        return part.reshape(TOK, HD)

    def wide(buf, i):
        return (buf[0, i] if i < YS else buf[1, :, i - YS]).reshape(2 * TOK, HD)

    def bounds(ch):
        lo, hi = ((0, NEAR), (NEAR, ZS))[ch]
        return lo, hi, slice(lo * 256, hi * 256), (hi - lo) * 256

    def scores(ch, tiles=range(TILES)):
        lo, hi, cols, n = bounds(ch)
        for i in tiles:
            lanes = slice(i * TOK, i * TOK + TOK)
            s = nt(kv[lo:hi, :, 0].reshape(n, HD), tile(qb, i)) * SCALE2
            s = s.reshape(hi - lo, 32, 8, TOK)
            peak = jnp.max(s, axis=1)
            w = jnp.exp2(s - peak[:, None])
            wt[cols, lanes] = w.reshape(n, TOK)
            pk[lo:hi, :, lanes] = peak
            ms[lo:hi, :, lanes] = jnp.sum(w, axis=1)

    def slopes(ch, tiles=range(TILES)):
        lo, hi, cols, n = bounds(ch)
        for i in tiles:
            lanes = slice(i * TOK, i * TOK + TOK)
            t = nt(kv[lo:hi, :, 1].reshape(n, HD), tile(gb, i))
            sl[cols, lanes] = t
            w = wt[cols, lanes].reshape(hi - lo, 32, 8, TOK)
            mo[lo:hi, :, lanes] = jnp.sum(w * t.reshape(hi - lo, 32, 8, TOK), axis=1)

    def local_mass():
        for i in range(TILES):
            lanes = slice(i * TOK, i * TOK + TOK)
            peak = pk[:, :, lanes]
            top = jnp.max(jnp.max(peak, axis=0), axis=0, keepdims=True)
            mass = jnp.sum(jnp.sum(ms[:, :, lanes] * jnp.exp2(peak - top[None]), axis=0), axis=0, keepdims=True)
            log_mass = top + jnp.log2(mass)
            cs[:, lanes] = log_mass
            st[0, i : i + 1, :] = log_mass

    def local_centre():
        for i in range(TILES):
            lanes = slice(i * TOK, i * TOK + TOK)
            factor = jnp.exp2(pk[:, :, lanes] - cs[:, lanes][None])
            st[1, i : i + 1, :] = jnp.sum(jnp.sum(mo[:, :, lanes] * factor, axis=0), axis=0, keepdims=True)

    def spread(src, landing, n, axis):
        return Group(*[(src.at[n], landing.at[n, d - 1], {axis: d}) for d in ring])

    def merge_mass(mine, landing, shares):
        logs = [mine[0]] + [landing[0, n] for n in range(3)]
        top = jnp.maximum(jnp.maximum(logs[0], logs[1]), jnp.maximum(logs[2], logs[3]))
        weights = [jnp.exp2(log - top) for log in logs]
        mass = weights[0] + weights[1] + weights[2] + weights[3]
        for n in range(4):
            shares[n] = weights[n] / mass
        return top + jnp.log2(mass)

    def merge_centre(mine, landing, shares):
        total = mine[1] * shares[0]
        for n in range(3):
            total = total + landing[1, n] * shares[n + 1]
        return total

    q_second.wait()
    keys_near.wait()
    scores(0, range(0, 8))
    keys_far.wait()
    keys_last = Group(*across(0, POS[4], POS[3], POS[-3]))
    scores(0, range(8, TILES))
    keys_last.wait()
    scores(1)
    local_mass()
    mass_x = spread(st, stx, 0, "dx")
    values_far.wait()
    values_last = Group(*across(1, POS[4], POS[3], POS[-3]))
    g_second.wait()
    values_near.wait()
    slopes(0)
    values_last.wait()
    slopes(1)
    local_centre()
    centre_x = spread(st, stx, 1, "dx")
    mass_x.wait()
    mid[0] = merge_mass(st, stx, share_x)
    mass_y = spread(mid, sty, 0, "dy")
    centre_x.wait()
    mid[1] = merge_centre(st, stx, share_x)
    centre_y = spread(mid, sty, 1, "dy")
    mass_y.wait()
    log_mass = merge_mass(mid, sty, share_y)
    for i in range(TILES):
        lanes = slice(i * TOK, i * TOK + TOK)
        fs[:, :, lanes] = jnp.exp2(pk[:, :, lanes] - log_mass[i : i + 1, :][None])

    def probabilities(p, cols, here):
        w = wt[cols, here].reshape(32, 8, 256)
        return (w * fs[p, :, here][None]).reshape(256, 256)

    def value_gradients(lo, hi):
        for p in range(lo, hi):
            dv = jnp.zeros((256, HD), F32)
            for i in range(ROWS // 256):
                here = slice(i * 256, i * 256 + 256)
                probs = probabilities(p, slice(p * 256, p * 256 + 256), here)
                dv = dv + nn(probs.astype(BF16), wide(gb, i))
            dvf[p] = dv.reshape(2, TOK, HD)

    def slope_gradients(p, kt, i):
        cols = slice(p * 256, p * 256 + 256)
        here = slice(i * 256, i * 256 + 256)
        ds = (probabilities(p, cols, here) * (sl[cols, here] - cs[:, here])).astype(BF16)
        dqt[:, here] += nn(kt, ds)
        return ds

    def key_gradients(lo, hi):
        for p in range(lo, hi):
            kt = kv[p, :, 0].reshape(256, HD).T
            dk = jnp.zeros((256, HD), F32)
            for i in range(ROWS // 256):
                dk = dk + nn(slope_gradients(p, kt, i), wide(qb, i))
            dkf[p] = dk.reshape(2, TOK, HD)

    def query_part(lo, hi, tiles):
        for p in range(lo, hi):
            kt = kv[p, :, 0].reshape(256, HD).T
            for i in tiles:
                dst[p * 256 : p * 256 + 256, i * 256 : i * 256 + 256] = slope_gradients(p, kt, i)

    def key_part(lo, hi):
        for p in range(lo, hi):
            dk = jnp.zeros((256, HD), F32)
            for i in range(ROWS // 256):
                dk = dk + nn(dst[p * 256 : p * 256 + 256, i * 256 : i * 256 + 256], wide(qb, i))
            dkf[p] = dk.reshape(2, TOK, HD)

    totals = (dkf, dvf)

    def pair(part, lo, hi):
        pair_out[part, lo:hi] = totals[part][lo:hi, 1].astype(BF16)
        return Group((pair_out.at[part, lo:hi], pair_in.at[part, lo:hi], dict(dc=1)))

    def whole(part, p):
        return totals[part][p, 0] + pair_in[part, p].astype(F32)

    def outward(part):
        for d in (4, 3, -3):
            red_out[part, POS[d]] = whole(part, POS[d]).astype(BF16)
        waits = []
        for n, way, span in ((0, 1, slice(0, HALF)), (1, -1, slice(HALF, TOK))):
            waits.append(Group(
                (red_out.at[part, POS[4], span], red_in.at[2, part, span], dict(dz=2 * way)),
                (red_out.at[part, POS[3 * way]], red_in.at[n, part], dict(dz=way)),
            ))
        return waits

    def direct(part, group):
        for d in (1, -1):
            red_out[part, POS[d]] = whole(part, POS[d]).astype(BF16)
        group.add(*[(red_out.at[part, POS[d]], red_in.at[n, part], dict(dz=d)) for n, d in ((3, 1), (4, -1))])

    def relay(part, waits, group):
        for n, d, span in ((0, 2, slice(0, HALF)), (1, -2, slice(HALF, TOK))):
            waits[n].wait()
            rest = slice(HALF, TOK) if n == 0 else slice(0, HALF)
            total = whole(part, POS[d]) + red_in[n, part].astype(F32)
            relay_out[n, part, span] = (total[span] + red_in[2, part, span].astype(F32)).astype(BF16)
            relay_out[n, part, rest] = total[rest].astype(BF16)
            group.add((relay_out.at[n, part], red_in.at[5 + n, part], dict(dz=d)))

    def owned(part):
        total = whole(part, 0)
        for n in (3, 4, 5, 6):
            total = total + red_in[n, part].astype(F32)
        return total

    def query_start(h):
        for j in range(TILES // 2):
            i = h * (TILES // 2) + j
            rows = dqt[:, i * TOK : i * TOK + TOK].T.astype(BF16)
            for b in range(2):
                ry, rx = j // 2, (j % 2) * 2 + b
                qa[h, ry, rx] = rows[b * HALF : b * HALF + HALF // 2]
                qc[h, rx, ry] = rows[b * HALF + HALF // 2 : b * HALF + HALF]
        return (
            Group(*[(qa.at[h, (y + d) % YS], qa_in.at[h, d - 1], dict(dy=d)) for d in ring]),
            Group(*[(qc.at[h, (x + d) % XS], qc_in.at[h, d - 1], dict(dx=d)) for d in ring]),
        )

    def four(mine, others):
        total = mine.astype(F32)
        for n in range(3):
            total = total + others[n].astype(F32)
        return total

    def query_second(h, waits):
        waits[0].wait()
        qa_mid[h] = four(qa[h, y], qa_in[h]).astype(BF16)
        group = Group(*[(qa_mid.at[h, (x + d) % XS], qa_fin.at[h, d - 1], dict(dx=d)) for d in ring])
        waits[1].wait()
        qc_mid[h] = four(qc[h, x], qc_in[h]).astype(BF16)
        group.add(*[(qc_mid.at[h, (y + d) % YS], qc_fin.at[h, d - 1], dict(dy=d)) for d in ring])
        return group

    def query_sum(h):
        return [four(qa_mid[h, x], qa_fin[h]), four(qc_mid[h, y], qc_fin[h])]

    value_gradients(NEAR, ZS)
    pair_far = pair(1, NEAR, ZS)
    value_gradients(3, NEAR)
    pair_mid = pair(1, 3, NEAR)
    pair_far.wait()
    values_out = outward(1)
    centre_y.wait()
    centre = merge_centre(mid, sty, share_y)
    for i in range(TILES):
        cs[:, i * TOK : i * TOK + TOK] = centre[i : i + 1, :]
    key_gradients(NEAR, ZS)
    pair_far = pair(0, NEAR, ZS)
    query_part(0, NEAR, range(0, YS))
    pair_far.wait()
    keys_out = outward(0)
    queries_out = [query_start(0)]
    query_part(0, NEAR, range(YS, 2 * YS))
    queries_out.append(query_start(1))
    pair_mid.wait()
    value_gradients(0, 3)
    pair_near = pair(1, 0, 3)
    values_in = Group()
    relay(1, values_out, values_in)
    key_part(0, 3)
    keys_near = pair(0, 0, 3)
    pair_near.wait()
    direct(1, values_in)
    key_part(3, NEAR)
    pair_mid = pair(0, 3, NEAR)
    keys_near.wait()
    keys_in = Group()
    direct(0, keys_in)
    pair_mid.wait()
    queries_in = [query_second(0, queries_out[0])]
    relay(0, keys_out, keys_in)
    queries_in.append(query_second(1, queries_out[1]))
    values_in.wait()
    out_ref[2] = turned(owned(1), bwd[...], 1).astype(BF16)
    queries_in[0].wait()
    queries_in[1].wait()
    dq = jnp.concatenate(query_sum(0) + query_sum(1), axis=0)
    out_ref[0] = (turned(dq, fwd[...], 1) * SCALE).astype(BF16)
    keys_in.wait()
    out_ref[1] = (turned(owned(0), bwd[...], 1) * SCALE).astype(BF16)
    for n, total in enumerate(sent):
        settle_bytes(total, send_sem.at[n])
    assert taken[0] <= RECV_SEMS and len(sent) <= SEND_SEMS


def per_device(queries, keys, values, out_grad, poses, pose_index):
    vmem = pl.BlockSpec(memory_space=pltpu.VMEM)
    smem = pl.BlockSpec(memory_space=pltpu.SMEM)

    def buf(*shape, kind=BF16):
        return pltpu.VMEM(shape, kind)

    part = HALF // 2
    out = pl.pallas_call(
        kernel,
        out_shape=jax.ShapeDtypeStruct((3, TOK, HD), BF16),
        in_specs=[vmem] * 4 + [smem] * 2,
        out_specs=vmem,
        scratch_shapes=[
            buf(2, YS, XS, HALF, HD), buf(2, XS, YS, HALF, HD), buf(ZS, 2, 2, TOK, HD),
            buf(COLS, ROWS, kind=F32), buf(COLS, ROWS, kind=F32),
            *[buf(ZS, 8, ROWS, kind=F32)] * 3,
            buf(2, TILES, TOK, kind=F32), buf(2, 3, TILES, TOK, kind=F32),
            buf(2, TILES, TOK, kind=F32), buf(2, 3, TILES, TOK, kind=F32),
            buf(4, TILES, TOK, kind=F32), buf(4, TILES, TOK, kind=F32),
            buf(ZS, 8, ROWS, kind=F32), buf(1, ROWS, kind=F32), buf(NEAR * 256, ROWS),
            buf(ZS, 2, TOK, HD, kind=F32), buf(ZS, 2, TOK, HD, kind=F32), buf(HD, ROWS, kind=F32),
            buf(2, ZS, TOK, HD), buf(2, ZS, TOK, HD),
            buf(2, ZS, TOK, HD), buf(2, 2, TOK, HD), buf(7, 2, TOK, HD),
            buf(2, YS, XS, part, HD), buf(2, 3, XS, part, HD), buf(2, XS, part, HD), buf(2, 3, part, HD),
            buf(2, XS, YS, part, HD), buf(2, 3, YS, part, HD), buf(2, YS, part, HD), buf(2, 3, part, HD),
            buf(HD, HD, kind=F32), buf(HD, HD, kind=F32),
            pltpu.SemaphoreType.DMA((SEND_SEMS,)), pltpu.SemaphoreType.DMA((RECV_SEMS,)),
        ],
        compiler_params=pltpu.CompilerParams(
            collective_id=0, has_side_effects=True, vmem_limit_bytes=58 * 2**20
        ),
    )(queries, keys, values, out_grad, jnp.transpose(poses, (1, 2, 0)), pose_index)
    return out[0:1], out[1:2], out[2:3]


def solution(mesh):
    block = P("view", "tok", None)
    return jax.shard_map(
        per_device, mesh=mesh, in_specs=(block,) * 4 + (P(), P()), out_specs=(block,) * 3, check_vma=False
    )
```

```python
import math

import jax
import jax.numpy as jnp
from jax import lax
from jax.experimental import pallas as pl
from jax.experimental.pallas import tpu as pltpu
from jax.sharding import PartitionSpec as P

F32 = jnp.float32
BF16 = jnp.bfloat16
MESH = pl.DeviceIdType.MESH
HD = 128
TOK = 128
XS, YS, ZS = 4, 4, 8
ROWS = XS * YS * TOK
COLS = ZS * 2 * TOK
SCALE = HD**-0.5
SCALE2 = SCALE / math.log(2.0)
RECV_SEMS = 46
SEND_SEMS = 4
BUCKET = 2**20
HALF = TOK // 2
LANES = ROWS // 2
TILES = ROWS // TOK
DIST = (0, 1, -1, 2, -2, 3, -3, 4)
POS = {d: p for p, d in enumerate(DIST)}
NEAR = 5


def nt(a, b):
    return lax.dot_general(a, b, (((1,), (1,)), ((), ())), preferred_element_type=F32)


def nn(a, b):
    return lax.dot_general(a, b, (((1,), (0,)), ((), ())), preferred_element_type=F32)


def turned(a, b, b_dim):
    return lax.dot_general(
        a, b, (((1,), (b_dim,)), ((), ())),
        precision=lax.Precision.HIGHEST, preferred_element_type=F32,
    )


def tables(poses, pose_index, view):
    row = pose_index[view]
    mat = [[poses[i, j, row] for j in range(4)] for i in range(4)]
    back = [[mat[i][j] for j in range(3)] + [mat[3][i]] for i in range(3)]
    back.append(
        [-(mat[0][j] * mat[0][3] + mat[1][j] * mat[1][3] + mat[2][j] * mat[2][3]) for j in range(3)]
        + [mat[3][3]]
    )
    i = lax.broadcasted_iota(jnp.int32, (HD, HD), 0)
    j = lax.broadcasted_iota(jnp.int32, (HD, HD), 1)
    place = jnp.where(i // 4 == j // 4, (i % 4) * 4 + j % 4, 16)
    forward = jnp.zeros((HD, HD), F32)
    backward = jnp.zeros((HD, HD), F32)
    for a in range(4):
        for b in range(4):
            here = place == 4 * a + b
            forward = jnp.where(here, mat[a][b], forward)
            backward = jnp.where(here, back[a][b], backward)
    return forward, backward


def kernel(
    q_ref, k_ref, v_ref, g_ref, poses, pose_index, out_ref,
    qb, gb, kv, wt, sl, pk, ms, mo, st, stx, mid, sty, share_x, share_y, fs, cs, dst, dkf, dvf, dqt,
    pair_out, pair_in, red_out, relay_out, red_in,
    qa, qa_in, qa_mid, qa_fin, qc, qc_in, qc_mid, qc_fin, fwd, bwd, send_sem, recv_sem,
):
    view = lax.axis_index("view")
    tok = lax.axis_index("tok")
    y = view // 2
    x = (tok // 16) * 2 + view % 2
    z = (tok // 2) % 8
    c = tok % 2
    taken = [0]
    sent = [0]
    ring = (1, 3, 2)

    def device(dx=0, dy=0, dz=0, dc=0):
        px, py, pz, pc = (x + dx) % XS, (y + dy) % YS, (z + dz + ZS) % ZS, (c + dc) % 2
        return (py * 2 + px % 2, ((px // 2) * ZS + pz) * 2 + pc)

    def amount(ref):
        return math.prod(ref.shape) * jnp.dtype(ref.dtype).itemsize

    def settle_bytes(total, sem):
        rows = total // (4 * HD)
        span = wt.at[:rows, :HD]
        pltpu.make_async_copy(span, span, sem).wait()

    class Group:
        def __init__(self, *sends):
            self.n = taken[0]
            self.total = 0
            taken[0] += 1
            self.add(*sends)

        def add(self, *sends):
            for src, dst, to in sends:
                size = amount(src)
                self.total += size
                if sent[-1] + size > BUCKET:
                    sent.append(0)
                sent[-1] += size
                pltpu.make_async_remote_copy(
                    src_ref=src, dst_ref=dst, send_sem=send_sem.at[len(sent) - 1], recv_sem=recv_sem.at[self.n],
                    device_id=device(**to), device_id_type=MESH,
                ).start()

        def wait(self):
            settle_bytes(self.total, recv_sem.at[self.n])

    barrier = pltpu.get_barrier_semaphore()
    peers = [dict(dx=d) for d in ring] + [dict(dy=d) for d in ring]
    peers += [dict(dz=d) for d in (1, -1, 2, -2)] + [dict(dc=1)]
    for peer in peers:
        pl.semaphore_signal(barrier, inc=1, device_id=device(**peer), device_id_type=MESH)

    forward, backward = tables(poses, pose_index, view)
    fwd[...] = forward
    bwd[...] = backward
    for ref, buf in ((q_ref, qb), (g_ref, gb)):
        own = turned(ref[0].astype(F32), forward, 0).astype(BF16)
        buf[0, y, x] = own[:HALF]
        buf[1, x, y] = own[HALF:]
    kv[0, 0, 0] = turned(k_ref[0].astype(F32), backward, 0).astype(BF16)
    kv[0, 0, 1] = turned(v_ref[0].astype(F32), backward, 0).astype(BF16)
    dqt[...] = jnp.zeros_like(dqt)
    pl.semaphore_wait(barrier, len(peers))

    def rows_first(buf):
        return (
            Group(*[(buf.at[0, y, x], buf.at[0, y, x], dict(dx=d)) for d in ring]),
            Group(*[(buf.at[1, x, y], buf.at[1, x, y], dict(dy=d)) for d in ring]),
        )

    def rows_second(buf, first):
        first[0].wait()
        group = Group(*[(buf.at[0, y], buf.at[0, y], dict(dy=d)) for d in ring])
        first[1].wait()
        group.add(*[(buf.at[1, x], buf.at[1, x], dict(dx=d)) for d in ring])
        return group

    def onward(part, p, to_p, distance, span=slice(None)):
        return (kv.at[p, 0, part, span], kv.at[to_p, 0, part, span], dict(dz=distance))

    def across(part, *places):
        return [(kv.at[p, 0, part], kv.at[p, 1, part], dict(dc=1)) for p in places]

    def columns_first(part):
        ahead = Group(onward(part, 0, POS[-2], 2))
        behind = Group(onward(part, 0, POS[2], -2))
        beside = Group(onward(part, 0, POS[-1], 1), onward(part, 0, POS[1], -1))
        return ahead, behind, beside

    def columns_second(part, first, near):
        far = None
        for way, span in ((1, slice(0, HALF)), (-1, slice(HALF, TOK))):
            first[0 if way == 1 else 1].wait()
            p = POS[-2 * way]
            sends = (onward(part, p, POS[4], 2 * way, span), onward(part, p, POS[-3 * way], way))
            if far is None:
                far = Group(*sends)
            else:
                far.add(*sends)
            near.add(*across(part, p))
        first[2].wait()
        near.add(*across(part, POS[1], POS[-1]))
        return far

    keys_first = columns_first(0)
    q_first = rows_first(qb)
    keys_near = Group(*across(0, 0))
    values_first = columns_first(1)
    g_first = rows_first(gb)
    values_near = Group(*across(1, 0))
    q_second = rows_second(qb, q_first)
    keys_far = columns_second(0, keys_first, keys_near)
    g_second = rows_second(gb, g_first)
    values_far = columns_second(1, values_first, values_near)

    def tile(buf, i):
        h, i = i // 8, i % 8
        ry, rx = i // 2, (i % 2) * 2
        part = buf[0, ry, rx : rx + 2] if h == 0 else buf[1, rx : rx + 2, ry]
        return part.reshape(TOK, HD)

    def wide(buf, i):
        return (buf[0, i] if i < YS else buf[1, :, i - YS]).reshape(2 * TOK, HD)

    def bounds(ch):
        lo, hi = ((0, NEAR), (NEAR, ZS))[ch]
        return lo, hi, slice(lo * 256, hi * 256), (hi - lo) * 256

    def scores(ch, tiles=range(TILES)):
        lo, hi, cols, n = bounds(ch)
        for i in tiles:
            lanes = slice(i * TOK, i * TOK + TOK)
            s = nt(kv[lo:hi, :, 0].reshape(n, HD), tile(qb, i)) * SCALE2
            s = s.reshape(hi - lo, 32, 8, TOK)
            peak = jnp.max(s, axis=1)
            w = jnp.exp2(s - peak[:, None])
            wt[cols, lanes] = w.reshape(n, TOK)
            pk[lo:hi, :, lanes] = peak
            ms[lo:hi, :, lanes] = jnp.sum(w, axis=1)

    def slopes(ch, tiles=range(TILES)):
        lo, hi, cols, n = bounds(ch)
        for i in tiles:
            lanes = slice(i * TOK, i * TOK + TOK)
            t = nt(kv[lo:hi, :, 1].reshape(n, HD), tile(gb, i))
            sl[cols, lanes] = t
            w = wt[cols, lanes].reshape(hi - lo, 32, 8, TOK)
            mo[lo:hi, :, lanes] = jnp.sum(w * t.reshape(hi - lo, 32, 8, TOK), axis=1)

    def local_mass():
        for i in range(TILES):
            lanes = slice(i * TOK, i * TOK + TOK)
            peak = pk[:, :, lanes]
            top = jnp.max(jnp.max(peak, axis=0), axis=0, keepdims=True)
            mass = jnp.sum(jnp.sum(ms[:, :, lanes] * jnp.exp2(peak - top[None]), axis=0), axis=0, keepdims=True)
            log_mass = top + jnp.log2(mass)
            cs[:, lanes] = log_mass
            st[0, i : i + 1, :] = log_mass

    def local_centre():
        for i in range(TILES):
            lanes = slice(i * TOK, i * TOK + TOK)
            factor = jnp.exp2(pk[:, :, lanes] - cs[:, lanes][None])
            st[1, i : i + 1, :] = jnp.sum(jnp.sum(mo[:, :, lanes] * factor, axis=0), axis=0, keepdims=True)

    def spread(src, landing, n, axis):
        return Group(*[(src.at[n], landing.at[n, d - 1], {axis: d}) for d in ring])

    def merge_mass(mine, landing, shares):
        logs = [mine[0]] + [landing[0, n] for n in range(3)]
        top = jnp.maximum(jnp.maximum(logs[0], logs[1]), jnp.maximum(logs[2], logs[3]))
        weights = [jnp.exp2(log - top) for log in logs]
        mass = weights[0] + weights[1] + weights[2] + weights[3]
        for n in range(4):
            shares[n] = weights[n] / mass
        return top + jnp.log2(mass)

    def merge_centre(mine, landing, shares):
        total = mine[1] * shares[0]
        for n in range(3):
            total = total + landing[1, n] * shares[n + 1]
        return total

    q_second.wait()
    keys_near.wait()
    scores(0, range(0, 8))
    keys_far.wait()
    keys_last = Group(*across(0, POS[4], POS[3], POS[-3]))
    scores(0, range(8, TILES))
    keys_last.wait()
    scores(1)
    local_mass()
    mass_x = spread(st, stx, 0, "dx")
    values_far.wait()
    values_last = Group(*across(1, POS[4], POS[3], POS[-3]))
    g_second.wait()
    values_near.wait()
    slopes(0)
    values_last.wait()
    slopes(1)
    local_centre()
    centre_x = spread(st, stx, 1, "dx")
    mass_x.wait()
    mid[0] = merge_mass(st, stx, share_x)
    mass_y = spread(mid, sty, 0, "dy")
    centre_x.wait()
    mid[1] = merge_centre(st, stx, share_x)
    centre_y = spread(mid, sty, 1, "dy")
    mass_y.wait()
    log_mass = merge_mass(mid, sty, share_y)
    for i in range(TILES):
        lanes = slice(i * TOK, i * TOK + TOK)
        fs[:, :, lanes] = jnp.exp2(pk[:, :, lanes] - log_mass[i : i + 1, :][None])

    def probabilities(p, cols, here):
        w = wt[cols, here].reshape(32, 8, 256)
        return (w * fs[p, :, here][None]).reshape(256, 256)

    def value_gradients(lo, hi):
        for p in range(lo, hi):
            dv = jnp.zeros((256, HD), F32)
            for i in range(ROWS // 256):
                here = slice(i * 256, i * 256 + 256)
                probs = probabilities(p, slice(p * 256, p * 256 + 256), here)
                dv = dv + nn(probs.astype(BF16), wide(gb, i))
            dvf[p] = dv.reshape(2, TOK, HD)

    def slope_gradients(p, kt, i):
        cols = slice(p * 256, p * 256 + 256)
        here = slice(i * 256, i * 256 + 256)
        ds = (probabilities(p, cols, here) * (sl[cols, here] - cs[:, here])).astype(BF16)
        dqt[:, here] += nn(kt, ds)
        return ds

    def key_gradients(lo, hi):
        for p in range(lo, hi):
            kt = kv[p, :, 0].reshape(256, HD).T
            dk = jnp.zeros((256, HD), F32)
            for i in range(ROWS // 256):
                dk = dk + nn(slope_gradients(p, kt, i), wide(qb, i))
            dkf[p] = dk.reshape(2, TOK, HD)

    def query_part(lo, hi, tiles):
        for p in range(lo, hi):
            kt = kv[p, :, 0].reshape(256, HD).T
            for i in tiles:
                dst[p * 256 : p * 256 + 256, i * 256 : i * 256 + 256] = slope_gradients(p, kt, i)

    def key_part(lo, hi):
        for p in range(lo, hi):
            dk = jnp.zeros((256, HD), F32)
            for i in range(ROWS // 256):
                dk = dk + nn(dst[p * 256 : p * 256 + 256, i * 256 : i * 256 + 256], wide(qb, i))
            dkf[p] = dk.reshape(2, TOK, HD)

    totals = (dkf, dvf)

    def pair(part, lo, hi):
        pair_out[part, lo:hi] = totals[part][lo:hi, 1].astype(BF16)
        return Group((pair_out.at[part, lo:hi], pair_in.at[part, lo:hi], dict(dc=1)))

    def whole(part, p):
        return totals[part][p, 0] + pair_in[part, p].astype(F32)

    def outward(part):
        for d in (4, 3, -3):
            red_out[part, POS[d]] = whole(part, POS[d]).astype(BF16)
        waits = []
        for n, way, span in ((0, 1, slice(0, HALF)), (1, -1, slice(HALF, TOK))):
            waits.append(Group(
                (red_out.at[part, POS[4], span], red_in.at[2, part, span], dict(dz=2 * way)),
                (red_out.at[part, POS[3 * way]], red_in.at[n, part], dict(dz=way)),
            ))
        return waits

    def direct(part, group):
        for d in (1, -1):
            red_out[part, POS[d]] = whole(part, POS[d]).astype(BF16)
        group.add(*[(red_out.at[part, POS[d]], red_in.at[n, part], dict(dz=d)) for n, d in ((3, 1), (4, -1))])

    def relay(part, waits, group):
        for n, d, span in ((0, 2, slice(0, HALF)), (1, -2, slice(HALF, TOK))):
            waits[n].wait()
            rest = slice(HALF, TOK) if n == 0 else slice(0, HALF)
            total = whole(part, POS[d]) + red_in[n, part].astype(F32)
            relay_out[n, part, span] = (total[span] + red_in[2, part, span].astype(F32)).astype(BF16)
            relay_out[n, part, rest] = total[rest].astype(BF16)
            group.add((relay_out.at[n, part], red_in.at[5 + n, part], dict(dz=d)))

    def owned(part):
        total = whole(part, 0)
        for n in (3, 4, 5, 6):
            total = total + red_in[n, part].astype(F32)
        return total

    def query_start(h):
        for j in range(TILES // 2):
            i = h * (TILES // 2) + j
            rows = dqt[:, i * TOK : i * TOK + TOK].T.astype(BF16)
            for b in range(2):
                ry, rx = j // 2, (j % 2) * 2 + b
                qa[h, ry, rx] = rows[b * HALF : b * HALF + HALF // 2]
                qc[h, rx, ry] = rows[b * HALF + HALF // 2 : b * HALF + HALF]
        return (
            Group(*[(qa.at[h, (y + d) % YS], qa_in.at[h, d - 1], dict(dy=d)) for d in ring]),
            Group(*[(qc.at[h, (x + d) % XS], qc_in.at[h, d - 1], dict(dx=d)) for d in ring]),
        )

    def four(mine, others):
        total = mine.astype(F32)
        for n in range(3):
            total = total + others[n].astype(F32)
        return total

    def query_second(h, waits):
        waits[0].wait()
        qa_mid[h] = four(qa[h, y], qa_in[h]).astype(BF16)
        group = Group(*[(qa_mid.at[h, (x + d) % XS], qa_fin.at[h, d - 1], dict(dx=d)) for d in ring])
        waits[1].wait()
        qc_mid[h] = four(qc[h, x], qc_in[h]).astype(BF16)
        group.add(*[(qc_mid.at[h, (y + d) % YS], qc_fin.at[h, d - 1], dict(dy=d)) for d in ring])
        return group

    def query_sum(h):
        return [four(qa_mid[h, x], qa_fin[h]), four(qc_mid[h, y], qc_fin[h])]

    value_gradients(NEAR, ZS)
    pair_far = pair(1, NEAR, ZS)
    value_gradients(3, NEAR)
    pair_mid = pair(1, 3, NEAR)
    pair_far.wait()
    values_out = outward(1)
    centre_y.wait()
    centre = merge_centre(mid, sty, share_y)
    for i in range(TILES):
        cs[:, i * TOK : i * TOK + TOK] = centre[i : i + 1, :]
    key_gradients(NEAR, ZS)
    pair_far = pair(0, NEAR, ZS)
    query_part(0, NEAR, range(0, YS))
    pair_far.wait()
    keys_out = outward(0)
    queries_out = [query_start(0)]
    query_part(0, NEAR, range(YS, 2 * YS))
    queries_out.append(query_start(1))
    pair_mid.wait()
    value_gradients(0, 3)
    pair_near = pair(1, 0, 3)
    values_in = Group()
    relay(1, values_out, values_in)
    key_part(0, 3)
    keys_near = pair(0, 0, 3)
    pair_near.wait()
    direct(1, values_in)
    queries_in = [query_second(0, queries_out[0])]
    key_part(3, NEAR)
    pair_mid = pair(0, 3, NEAR)
    keys_near.wait()
    keys_in = Group()
    direct(0, keys_in)
    pair_mid.wait()
    relay(0, keys_out, keys_in)
    queries_in.append(query_second(1, queries_out[1]))
    values_in.wait()
    out_ref[2] = turned(owned(1), bwd[...], 1).astype(BF16)
    queries_in[0].wait()
    queries_in[1].wait()
    dq = jnp.concatenate(query_sum(0) + query_sum(1), axis=0)
    out_ref[0] = (turned(dq, fwd[...], 1) * SCALE).astype(BF16)
    keys_in.wait()
    out_ref[1] = (turned(owned(0), bwd[...], 1) * SCALE).astype(BF16)
    for n, total in enumerate(sent):
        settle_bytes(total, send_sem.at[n])
    assert taken[0] <= RECV_SEMS and len(sent) <= SEND_SEMS


def per_device(queries, keys, values, out_grad, poses, pose_index):
    vmem = pl.BlockSpec(memory_space=pltpu.VMEM)
    smem = pl.BlockSpec(memory_space=pltpu.SMEM)

    def buf(*shape, kind=BF16):
        return pltpu.VMEM(shape, kind)

    part = HALF // 2
    out = pl.pallas_call(
        kernel,
        out_shape=jax.ShapeDtypeStruct((3, TOK, HD), BF16),
        in_specs=[vmem] * 4 + [smem] * 2,
        out_specs=vmem,
        scratch_shapes=[
            buf(2, YS, XS, HALF, HD), buf(2, XS, YS, HALF, HD), buf(ZS, 2, 2, TOK, HD),
            buf(COLS, ROWS, kind=F32), buf(COLS, ROWS, kind=F32),
            *[buf(ZS, 8, ROWS, kind=F32)] * 3,
            buf(2, TILES, TOK, kind=F32), buf(2, 3, TILES, TOK, kind=F32),
            buf(2, TILES, TOK, kind=F32), buf(2, 3, TILES, TOK, kind=F32),
            buf(4, TILES, TOK, kind=F32), buf(4, TILES, TOK, kind=F32),
            buf(ZS, 8, ROWS, kind=F32), buf(1, ROWS, kind=F32), buf(NEAR * 256, ROWS),
            buf(ZS, 2, TOK, HD, kind=F32), buf(ZS, 2, TOK, HD, kind=F32), buf(HD, ROWS, kind=F32),
            buf(2, ZS, TOK, HD), buf(2, ZS, TOK, HD),
            buf(2, ZS, TOK, HD), buf(2, 2, TOK, HD), buf(7, 2, TOK, HD),
            buf(2, YS, XS, part, HD), buf(2, 3, XS, part, HD), buf(2, XS, part, HD), buf(2, 3, part, HD),
            buf(2, XS, YS, part, HD), buf(2, 3, YS, part, HD), buf(2, YS, part, HD), buf(2, 3, part, HD),
            buf(HD, HD, kind=F32), buf(HD, HD, kind=F32),
            pltpu.SemaphoreType.DMA((SEND_SEMS,)), pltpu.SemaphoreType.DMA((RECV_SEMS,)),
        ],
        compiler_params=pltpu.CompilerParams(
            collective_id=0, has_side_effects=True, vmem_limit_bytes=58 * 2**20
        ),
    )(queries, keys, values, out_grad, jnp.transpose(poses, (1, 2, 0)), pose_index)
    return out[0:1], out[1:2], out[2:3]


def solution(mesh):
    block = P("view", "tok", None)
    return jax.shard_map(
        per_device, mesh=mesh, in_specs=(block,) * 4 + (P(), P()), out_specs=(block,) * 3, check_vma=False
    )
```
